128 devices in a mesh: hst: 16 (over y, x), chip: 8 (over z, core).
Axes of the slice: x: 4, y: 4, z: 4, core: 2. Of those that a mesh axis runs over, the one named last changes fastest.
Arguments:
- tile_data: bfloat16 [4096, 512, 512], P(('hst', 'chip')), may hold values from -0.09375 to 0.09375
- tile_col: int32 [4096], P(('hst', 'chip')), may hold values from 0 to 127, as said below
- live_count: int32 [128], P(('hst', 'chip')), may hold values from 16 to 32, as said below
- degree: int32 [65536], P(('hst', 'chip')), may hold values from 1 to 100
- start_basis: bfloat16 [65536, 128], P(('hst', 'chip')), may hold values from -6 to 6
Outputs:
- leading_basis: float32 [65536, 128], P(('hst', 'chip'))
- factor: float32 [128, 128], replicated
The draws below stay inside these ranges and needn't reach their ends.
Inputs may be any that keep to these rules, and one draw needn't show every extreme that they name: `tile_col`: slot 0 of every row block names that block itself. `live_count`: some row block has all 32 slots live in every draw.
All inputs are finite; a program needn't handle non-finite values.
Results may differ from the reference program's by a relative error of at most 0.019.
Values may be sent and summed in bfloat16 or wider, within the bound.
A program may use at most 128 MiB of HBM per device.

```python
import jax
import jax.numpy as jnp
from jax import lax

BLK = 512
K = 128
TILE_DEV = 32
TILES = 4096
ITEMS = 65536


def draw_live_count(key, part):
    key = jax.random.fold_in(key, 11)
    block_total = TILES // TILE_DEV
    key_one, key_two, key_three = jax.random.split(key, 3)
    first_draw = jax.random.randint(key_one, (block_total,), 1, TILE_DEV + 1)
    second_draw = jax.random.randint(key_two, (block_total,), 1, TILE_DEV + 1)
    counts = jnp.maximum(TILE_DEV // 2, first_draw * second_draw // TILE_DEV)
    full_block = jax.random.randint(key_three, (), 0, block_total)
    return jnp.where(jnp.arange(block_total) == full_block, TILE_DEV, counts).astype(jnp.int32)


def draw_tile_col(key, part):
    key = jax.random.fold_in(key, 12)
    block_total = TILES // TILE_DEV
    key_one, key_two, key_three, key_four = jax.random.split(key, 4)
    first_draw = jax.random.randint(key_one, (block_total, TILE_DEV), 0, block_total)
    second_draw = jax.random.randint(key_two, (block_total, TILE_DEV), 0, block_total)
    leaning = first_draw * second_draw // block_total
    multiplier = 2 * jax.random.randint(key_three, (), 0, block_total // 2) + 1
    offset = jax.random.randint(key_four, (), 0, block_total)
    mapped = (leaning * multiplier + offset) % block_total
    own_block = jnp.arange(block_total)[:, None] + jnp.zeros((1, TILE_DEV), jnp.int32)
    slot_index = jnp.arange(TILE_DEV)[None, :] + jnp.zeros((block_total, 1), jnp.int32)
    return jnp.where(slot_index == 0, own_block, mapped).reshape(-1).astype(jnp.int32)


def plant(entries, rng, low, largest):
    shape = entries.shape
    index_at = [jax.random.randint(jax.random.fold_in(rng, axis), (), 0, shape[axis]) for axis in range(len(shape))]
    entries = entries.at[tuple(index_at)].set(low)
    longest = shape.index(max(shape))
    index_at[longest] = (index_at[longest] + 1) % shape[longest]
    return entries.at[tuple(index_at)].set(largest)


def block_levels(stream_key, dims, shards, least, largest):
    loudness = 1.0
    for dim, blocks in shards:
        draws = jax.random.uniform(jax.random.fold_in(jax.random.fold_in(stream_key, 6), dim), (blocks,), jnp.float32, least / len(shards), largest / len(shards))
        loudness = loudness * jnp.repeat(jnp.exp(draws), dims[dim] // blocks).reshape((-1,) + (1,) * (len(dims) - 1 - dim))
    return loudness


def normal_values(rng, shape, width, most, cuts=(), kind=jnp.bfloat16):
    entries = jax.random.normal(rng, shape, jnp.float32) * width
    if len(cuts) > 0:
        entries = block_levels(rng, shape, cuts, -0.22, 0.18) * entries
    return jnp.clip(entries, min=-most, max=most).astype(kind)


def setup_inputs(seed: int = 0) -> dict:
    keys = jax.random.split(jax.random.key(seed), 6)
    return {
        "tile_data": normal_values(keys[0], (TILES, BLK, BLK), (BLK * 8) ** -0.5, 0.09375, ((0, 128),)),
        "tile_col": draw_tile_col(jax.random.fold_in(keys[5], 71), 0),
        "live_count": draw_live_count(jax.random.fold_in(keys[5], 71), 0),
        "degree": plant(jax.random.randint(keys[3], (ITEMS,), 1, 101), jax.random.fold_in(keys[3], 1), 1, 100).astype(jnp.int32),
        "start_basis": normal_values(keys[4], (ITEMS, K), 1.0, 6.0, ((0, 128),)),
    }


def apply_matrix(tile_data, tile_col, live_count, scaled, row_scale):
    block_total = live_count.shape[0]
    blocks = scaled.reshape(block_total, BLK, K)
    tiles_grouped = tile_data.reshape(block_total, TILE_DEV, BLK, BLK)
    cols_grouped = tile_col.reshape(block_total, TILE_DEV)

    def device_rows(inputs):
        tiles_one, cols_one, count_one = inputs
        picked = blocks[cols_one].astype(jnp.float32)
        living = (jnp.arange(TILE_DEV, dtype=jnp.int32) < count_one).astype(jnp.float32)
        product = jnp.einsum('sij,sjk->sik', tiles_one.astype(jnp.float32), picked, precision=lax.Precision.HIGHEST)
        return jnp.einsum('s,sik->ik', living, product, precision=lax.Precision.HIGHEST)
    row_sums = lax.map(device_rows, (tiles_grouped, cols_grouped, live_count))
    return row_sums.reshape(block_total * BLK, K) * row_scale[:, None]

def factor_inverse(gram_matrix):
    lower_factor = jnp.linalg.cholesky(gram_matrix)
    identity = jnp.eye(gram_matrix.shape[0], dtype=jnp.float32)
    inverse = lax.linalg.triangular_solve(lower_factor, identity, left_side=True, lower=True)
    return (lower_factor, inverse)

def reference(tile_data, tile_col, live_count, degree, start_basis):
    row_scale = 1.0 / jnp.sqrt(degree.astype(jnp.float32))
    start_scaled = (row_scale[:, None] * start_basis.astype(jnp.float32)).astype(jnp.bfloat16)
    first_image = apply_matrix(tile_data, tile_col, live_count, start_scaled, row_scale)
    first_gram = jnp.dot(first_image.T, first_image, precision=lax.Precision.HIGHEST) / ITEMS
    lower_one, inverse_one = factor_inverse(first_gram)
    mid_scaled = (row_scale[:, None] * first_image).astype(jnp.bfloat16)
    raw_second = apply_matrix(tile_data, tile_col, live_count, mid_scaled, row_scale)
    second = jnp.dot(raw_second, inverse_one.T, precision=lax.Precision.HIGHEST)
    second_gram = jnp.dot(second.T, second, precision=lax.Precision.HIGHEST) / ITEMS
    factor, inverse_two = factor_inverse(second_gram)
    leading_basis = jnp.dot(second, inverse_two.T, precision=lax.Precision.HIGHEST)
    return (leading_basis, factor)
```

```python
import functools

import jax
import jax.numpy as jnp
from jax import lax
from jax.experimental import pallas as pl
from jax.experimental.pallas import tpu as pltpu
from jax.sharding import PartitionSpec as P

BLK = 512
K = 128
SLOTS = 32
RING = 4
WAVES = 2
DEPTH = BLK // WAVES
MESH = pl.DeviceIdType.MESH
HIGHEST = lax.Precision.HIGHEST
ALL = pl.ds(0, RING)
HALVES = ((1, pl.ds(0, 2)), (3, pl.ds(2, 2)))
ORDER = ((1, 0, 2), (0, 2, 1), (2, 1, 0))
ROWS = (((0, 96), (96, 80), (176, 80)), ((0, 80), (80, 80), (160, 96)))
GRAM_ROWS = ((0, 24), (24, 24), (48, 16))
COPIES = 280
SUMS = 40


def position():
    host, chip = lax.axis_index("hst"), lax.axis_index("chip")
    return (host // RING, lax.rem(host, RING), chip // 2), lax.rem(chip, 2)


class Links:
    def __init__(self, send, recv):
        self.send, self.recv = send, recv
        self.pos, self.core = position()
        self.ids, self.started = {}, []

    def at(self, axis, delta):
        return lax.rem(self.pos[axis] + delta, RING)

    def device(self, axis=None, delta=0):
        place = list(self.pos)
        core = self.core
        if axis is None:
            core = 1 - core
        else:
            place[axis] = self.at(axis, delta)
        return (place[0] * RING + place[1], place[2] * 2 + core)

    def copy(self, key, src, dst, device):
        index = self.ids.setdefault(key, len(self.ids))
        return pltpu.make_async_remote_copy(
            src_ref=src,
            dst_ref=dst,
            send_sem=self.send.at[index],
            recv_sem=self.recv.at[index],
            device_id=device,
            device_id_type=MESH,
        )

    def start(self, key, src, dst, device):
        copy = self.copy(key, src, dst, device)
        copy.start()
        self.started.append(copy)

    def wait(self, key, dst):
        self.copy(key, dst, dst, self.device()).wait_recv()

    def finish(self):
        for copy in self.started:
            copy.wait_send()
        self.started = []


class Gather(Links):
    def __init__(self, waves, send, recv):
        super().__init__(send, recv)
        self.waves = waves

    def view(self, w, t, axes, core=None):
        first, rows = ROWS[w][t]
        index = [axes.get(axis, self.pos[axis]) for axis in range(3)]
        core = self.core if core is None else core
        return self.waves[w].at[index[0], index[1], index[2], core, pl.ds(first, rows), :]

    def push(self, key, view, device):
        self.start(key, view, view, device)

    def line(self, t, second=None, third=None, half=ALL):
        axes = {ORDER[t][0]: half}
        if second is not None:
            axes[ORDER[t][1]] = second
        if third is not None:
            axes[ORDER[t][2]] = third
        return axes

    def seconds(self, t):
        return [self.at(ORDER[t][1], delta) for delta in (0, 3, 1, 2)]

    def first_start(self, w, t):
        for delta in (1, 3, 2):
            self.push((w, t, 1, delta), self.view(w, t, {}), self.device(ORDER[t][0], delta))

    def third_line(self, w, t, j):
        view = self.view(w, t, self.line(t, self.seconds(t)[j]))
        for delta in (1, 3):
            self.push((w, t, 3, delta, j), view, self.device(ORDER[t][2], delta))
        self.sibling(w, t, j, 0)

    def sibling(self, w, t, j, away):
        axes = self.line(t, self.seconds(t)[j], self.at(ORDER[t][2], 4 - away))
        self.push((w, t, "s", j, away), self.view(w, t, axes), self.device())

    def first_end(self, w, t):
        axis = ORDER[t][0]
        for delta in (1, 3, 2):
            self.wait((w, t, 1, delta), self.view(w, t, {axis: self.at(axis, 4 - delta)}))
        view = self.view(w, t, self.line(t))
        for delta in (1, 3):
            self.push((w, t, 2, delta), view, self.device(ORDER[t][1], delta))
        self.third_line(w, t, 0)

    def second_pass(self, w, t, k):
        delta, half = HALVES[k]
        source = self.seconds(t)[k + 1]
        self.wait((w, t, 2, delta), self.view(w, t, self.line(t, source)))
        view = self.view(w, t, self.line(t, source, half=half))
        self.push((w, t, 2, delta, "f"), view, self.device(ORDER[t][1], delta))
        self.third_line(w, t, k + 1)

    def second_end(self, w, t):
        source = self.seconds(t)[3]
        for delta, half in HALVES:
            self.wait((w, t, 2, delta, "f"), self.view(w, t, self.line(t, source, half=half)))
        self.third_line(w, t, 3)

    def third_pass(self, w, t, j):
        axis, source = ORDER[t][2], self.seconds(t)[j]
        for delta, half in HALVES:
            origin = self.at(axis, 4 - delta)
            self.wait((w, t, 3, delta, j), self.view(w, t, self.line(t, source, origin)))
            view = self.view(w, t, self.line(t, source, origin, half=half))
            self.push((w, t, 3, delta, j, "f"), view, self.device(axis, delta))
            self.sibling(w, t, j, delta)

    def third_end(self, w, t, j):
        axis, source = ORDER[t][2], self.seconds(t)[j]
        for delta, half in HALVES:
            view = self.view(w, t, self.line(t, source, self.at(axis, 2), half=half))
            self.wait((w, t, 3, delta, j, "f"), view)
        self.sibling(w, t, j, 2)

    def sibling_end(self, w):
        for t in range(3):
            for j in range(4):
                for away in range(4):
                    axes = self.line(t, self.seconds(t)[j], self.at(ORDER[t][2], 4 - away))
                    self.wait((w, t, "s", j, away), self.view(w, t, axes, core=1 - self.core))

    def events(self):
        plan = [(self.first_start,), (self.first_end,), (self.second_pass, 0), (self.second_pass, 1)]
        plan += [(self.second_end,), (self.third_pass, 0), (self.third_pass, 1), (self.third_end, 0)]
        plan += [(self.third_pass, 2), (self.third_end, 1), (self.third_pass, 3), (self.third_end, 2)]
        plan += [(self.third_end, 3)]
        for step, *more in plan:
            for w in range(WAVES):
                for t in range(3):
                    yield functools.partial(step, w, t, *more)


class Sum(Links):
    def __init__(self, sibling_half, stages, total, send, recv):
        super().__init__(send, recv)
        self.sibling_half, self.stages, self.total = sibling_half, stages, total
        self.half = K // 2

    def rows(self, core):
        return pl.ds(pl.multiple_of(core * self.half, self.half), self.half)

    def begin(self, matrix):
        self.matrix = matrix
        self.start("s", matrix.at[self.rows(1 - self.core)], self.sibling_half, self.device())

    def stage_start(self, stage, value):
        for t in range(3):
            first, rows = GRAM_ROWS[t]
            axis = ORDER[t][stage]
            own = self.stages.at[stage, self.pos[axis], pl.ds(first, rows)]
            own[...] = value[first : first + rows]
            for delta in (2, 1, 3):
                self.push((stage, t, delta), own, self.device(axis, delta))

    def push(self, key, view, device):
        self.start(key, view, view, device)

    def stage_end(self, stage):
        parts = []
        for t in range(3):
            first, rows = GRAM_ROWS[t]
            axis = ORDER[t][stage]
            for delta in (1, 3, 2):
                view = self.stages.at[stage, self.at(axis, 4 - delta), pl.ds(first, rows)]
                self.wait((stage, t, delta), view)
            slots = [self.stages[stage, p, first : first + rows] for p in range(RING)]
            parts.append((slots[0] + slots[1]) + (slots[2] + slots[3]))
        return jnp.concatenate(parts, axis=0)

    def step_one(self):
        self.wait("s", self.sibling_half)
        self.stage_start(0, self.matrix[self.rows(self.core)] + self.sibling_half[...])

    def step_two(self):
        self.stage_start(1, self.stage_end(0))

    def step_three(self):
        self.stage_start(2, self.stage_end(1))

    def step_four(self):
        mine = self.total.at[self.rows(self.core)]
        mine[...] = self.stage_end(2)
        self.start("e", mine, mine, self.device())

    def step_five(self):
        self.wait("e", self.total.at[self.rows(1 - self.core)])


def product(left, right, left_dim, right_dim):
    dims = (((left_dim,), (right_dim,)), ((), ()))
    return lax.dot_general(left, right, dims, precision=HIGHEST, preferred_element_type=jnp.float32)


def factor_inverse(matrix, panel=32, pivots=8):
    ids = [lax.broadcasted_iota(jnp.int32, (K, K), dim) for dim in (0, 1)]
    side = jnp.where(ids[0] == ids[1], 1.0, 0.0)
    row = lax.broadcasted_iota(jnp.int32, (panel, K), 0)
    lane = lax.broadcasted_iota(jnp.int32, (panel, K), 1)
    uppers, inverses = [], []
    for first in range(0, K, panel):
        a, w = matrix[:panel], side[:panel]
        for j in range(0, panel, pivots):
            span = range(pivots)
            cols = [
                jnp.broadcast_to(a[:, first + j + q : first + j + q + 1], (panel, K)) for q in span
            ]
            row_a = [a[j + q : j + q + 1] for q in span]
            row_w = [w[j + q : j + q + 1] for q in span]
            small = [[cols[k][j + q : j + q + 1] for k in span] for q in span]
            for q in span:
                inverse = 1.0 / small[q][q]
                ratio = {k: small[q][k] * inverse for k in range(q + 1, pivots)}
                for k in range(q + 1, pivots):
                    for m in range(k, pivots):
                        small[k][m] = small[k][m] - ratio[k] * small[q][m]
                    row_a[k] = row_a[k] - ratio[k] * row_a[q]
                    row_w[k] = row_w[k] - ratio[k] * row_w[q]
                weight = jnp.where(row > j + q, cols[q], 0.0) * inverse
                for k in range(q + 1, pivots):
                    cols[k] = cols[k] - cols[q] * ratio[k]
                a = a - weight * row_a[q]
                w = w - weight * row_w[q]
        diagonal = jnp.sum(jnp.where(lane == row + first, a, 0.0), axis=1, keepdims=True)
        scale = lax.rsqrt(diagonal)
        a = jnp.where(lane >= row + first, a * scale, 0.0)
        w = w * scale
        uppers.append(a)
        inverses.append(w)
        if first + panel < K:
            rest = a[:, first + panel :]
            matrix = matrix[panel:] - product(rest, a, 0, 0)
            side = side[panel:] - product(rest, w, 0, 0)
    return jnp.concatenate(uppers, axis=0), jnp.concatenate(inverses, axis=0)


def kernel(
    cols,
    live,
    tiles_hbm,
    degree,
    basis,
    leading,
    factor,
    tiles,
    a0,
    a1,
    b0,
    b1,
    scale,
    total,
    gram,
    inverse,
    half_one,
    stages_one,
    sum_one,
    half_two,
    stages_two,
    sum_two,
    tile_sem,
    send_a,
    recv_a,
    send_b,
    recv_b,
    send_g,
    recv_g,
    send_h,
    recv_h,
):
    items = float(BLK * 2 * RING**3)
    loads = [
        pltpu.make_async_copy(
            tiles_hbm.at[pl.ds(8 * i, 8)], tiles.at[pl.ds(8 * i, 8)], tile_sem.at[i]
        )
        for i in range(4)
    ]
    first = Gather((a0, a1), send_a, recv_a)
    second = Gather((b0, b1), send_b, recv_b)
    gram_one = Sum(half_one, stages_one, sum_one, send_g, recv_g)
    gram_two = Sum(half_two, stages_two, sum_two, send_h, recv_h)
    pos, core = first.pos, first.core

    barrier = pltpu.get_barrier_semaphore()
    near = [first.device()] + [first.device(axis, d) for axis in range(3) for d in (1, 2, 3)]
    for device in near:
        pl.semaphore_signal(barrier, inc=1, device_id=device, device_id_type=MESH)
    for load in loads:
        load.start()

    for i in range(BLK // K):
        row_scale = 1.0 / jnp.sqrt(degree[pl.ds(i * K, K)].astype(jnp.float32))
        scale[pl.ds(i * K, K)] = jnp.broadcast_to(row_scale.reshape(1, K), (K, K)).T

    def place(waves, w, value):
        waves[w][pos[0], pos[1], pos[2], core] = value.astype(jnp.bfloat16)

    for w in range(WAVES):
        rows = pl.ds(w * DEPTH, DEPTH)
        place((a0, a1), w, scale[rows] * basis[rows].astype(jnp.float32))
    pl.semaphore_wait(barrier, len(near))

    def multiply(wave, w):
        depth = pl.ds(w * DEPTH, DEPTH)
        if w == 0:
            total[...] = jnp.zeros_like(total)

        @pl.loop(0, SLOTS // 4)
        def _(group):
            parts = []
            for u in range(4):
                slot = group * 4 + u
                col = cols[slot]
                picked = wave[col // 32, lax.rem(col // 8, 4), lax.rem(col // 2, 4), lax.rem(col, 2)]
                picked = jnp.where(slot < live[0], picked, jnp.zeros_like(picked))
                parts.append(
                    jnp.dot(tiles[slot, :, depth], picked, preferred_element_type=jnp.float32)
                )
            total[...] += (parts[0] + parts[1]) + (parts[2] + parts[3])

    for event in first.events():
        event()
    for load in loads:
        load.wait()
    for w in range(WAVES):
        first.sibling_end(w)
        multiply((a0, a1)[w], w)
    for w in range(WAVES):
        rows = pl.ds(w * DEPTH, DEPTH)
        image = total[rows] * scale[rows]
        total[rows] = image
        place((b0, b1), w, scale[rows] * image)

    events = list(second.events())
    for event in events[:12]:
        event()
    image = total[...]
    gram[...] = product(image, image, 0, 0) * (1.0 / items)
    gram_one.begin(gram)
    for event in events[12:24]:
        event()
    gram_one.step_one()
    for event in events[24:30]:
        event()
    gram_one.step_two()
    for event in events[30:36]:
        event()
    gram_one.step_three()
    for event in events[36:42]:
        event()
    gram_one.step_four()
    for event in events[42:48]:
        event()
    gram_one.step_five()
    _, inverse[...] = factor_inverse(sum_one[...])
    for event in events[48:]:
        event()
    for w in range(WAVES):
        second.sibling_end(w)
        multiply((b0, b1)[w], w)
    raw = total[...] * scale[...]
    image = product(raw, inverse[...], 1, 1)
    total[...] = image
    gram_one.finish()
    gram[...] = product(image, image, 0, 0) * (1.0 / items)
    gram_two.begin(gram)
    gram_two.step_one()
    gram_two.step_two()
    gram_two.step_three()
    gram_two.step_four()
    gram_two.step_five()
    upper, inverse[...] = factor_inverse(sum_two[...])
    factor[...] = upper.T
    leading[...] = product(total[...], inverse[...], 1, 1)
    first.finish()
    second.finish()
    gram_two.finish()


def local(tile_data, tile_col, live_count, degree, start_basis):
    vmem, smem = pl.BlockSpec(memory_space=pltpu.VMEM), pl.BlockSpec(memory_space=pltpu.SMEM)
    wave = pltpu.VMEM((RING, RING, RING, 2, DEPTH, K), jnp.bfloat16)
    sums = [
        pltpu.VMEM((K // 2, K), jnp.float32),
        pltpu.VMEM((3, RING, K // 2, K), jnp.float32),
        pltpu.VMEM((K, K), jnp.float32),
    ]
    dma = pltpu.SemaphoreType.DMA
    return pl.pallas_call(
        kernel,
        out_shape=(
            jax.ShapeDtypeStruct((BLK, K), jnp.float32),
            jax.ShapeDtypeStruct((K, K), jnp.float32),
        ),
        in_specs=[smem, smem, pl.BlockSpec(memory_space=pl.ANY), vmem, vmem],
        out_specs=(vmem, vmem),
        scratch_shapes=[
            pltpu.VMEM((SLOTS, BLK, BLK), jnp.bfloat16),
            wave,
            wave,
            wave,
            wave,
            pltpu.VMEM((BLK, K), jnp.float32),
            pltpu.VMEM((BLK, K), jnp.float32),
            pltpu.VMEM((K, K), jnp.float32),
            pltpu.VMEM((K, K), jnp.float32),
            *sums,
            *sums,
            dma((4,)),
            dma((COPIES,)),
            dma((COPIES,)),
            dma((COPIES,)),
            dma((COPIES,)),
            dma((SUMS,)),
            dma((SUMS,)),
            dma((SUMS,)),
            dma((SUMS,)),
        ],
        compiler_params=pltpu.CompilerParams(
            collective_id=0, has_side_effects=True, vmem_limit_bytes=58 * 2**20
        ),
        name="subspace_iteration",
    )(tile_col, live_count, tile_data, degree, start_basis)


def solution(mesh):
    placed = (
        P(("hst", "chip"), None, None),
        P(("hst", "chip")),
        P(("hst", "chip")),
        P(("hst", "chip")),
        P(("hst", "chip"), None),
    )
    return jax.shard_map(
        local,
        mesh=mesh,
        in_specs=placed,
        out_specs=(P(("hst", "chip"), None), P()),
        check_vma=False,
    )
```

```python
import functools

import jax
import jax.numpy as jnp
from jax import lax
from jax.experimental import pallas as pl
from jax.experimental.pallas import tpu as pltpu
from jax.sharding import PartitionSpec as P

BLK = 512
K = 128
SLOTS = 32
RING = 4
WAVES = 2
DEPTH = BLK // WAVES
MESH = pl.DeviceIdType.MESH
HIGHEST = lax.Precision.HIGHEST
ALL = pl.ds(0, RING)
HALVES = ((1, pl.ds(0, 2)), (3, pl.ds(2, 2)))
ORDER = ((1, 0, 2), (0, 2, 1), (2, 1, 0))
ROWS = (((0, 96), (96, 80), (176, 80)), ((0, 80), (80, 80), (160, 96)))
GRAM_ROWS = ((0, 24), (24, 24), (48, 16))
COPIES = 240
SUMS = 40
GROUP = 16
WHOLE_ONE = ((False, False, False), (True, True, False))
WHOLE_TWO = ((False, False, False), (True, True, False))
ROUND_ONE = (
    ("first", 1), ("first", 0), ("line", 1), ("line", 0), ("plane", 1, 0), ("plane", 0, 0),
    ("plane", 0, 1), ("plane", 1, 1), ("planed", 0), ("pass", 0, 0), ("share", 0, 0),
    ("pass", 0, 1), ("pass", 0, 2), ("pass", 0, 3), ("planed", 1), ("pass", 1, 0), ("far", 0, 0),
    ("far", 0, 1), ("pass", 1, 1), ("pass", 1, 2), ("share", 0, 1), ("far", 0, 2), ("far", 0, 3),
    ("share", 1, 0), ("share", 0, 3), ("share", 0, 2), ("pass", 1, 3), ("loaded",),
    ("multiply", 0, 0, 1), ("far", 1, 0), ("far", 1, 1), ("multiply", 0, 1, 2), ("far", 1, 2),
    ("far", 1, 3), ("share", 1, 1), ("share", 1, 3), ("share", 1, 2),
)
ROUND_TWO = (
    ("first", 0), ("half",), ("first", 1), ("line", 0), ("gram",), ("sum", 0), ("line", 1),
    ("sum", 1), ("plane", 0, 0), ("plane", 0, 1), ("sum", 2), ("plane", 1, 0), ("plane", 1, 1),
    ("planed", 0), ("pass", 0, 0), ("sum", 3), ("pass", 0, 1), ("pass", 0, 2), ("sum", 4),
    ("eliminate", 0), ("eliminate", 1), ("eliminate", 2), ("eliminate", 3), ("pass", 0, 3),
    ("planed", 1), ("share", 0, 0), ("pass", 1, 0), ("far", 0, 0), ("pass", 1, 1), ("far", 0, 1),
    ("share", 0, 1), ("far", 0, 2), ("far", 0, 3), ("share", 0, 3), ("pass", 1, 2), ("share", 0, 2),
    ("pass", 1, 3), ("multiply", 0, 0, 1), ("far", 1, 0), ("far", 1, 1), ("multiply", 0, 1, 2),
    ("far", 1, 2), ("far", 1, 3), ("share", 1, 0), ("share", 1, 1), ("share", 1, 3),
    ("share", 1, 2), ("multiply", 1, 0, 2),
)


def position():
    host, chip = lax.axis_index("hst"), lax.axis_index("chip")
    return (host // RING, lax.rem(host, RING), chip // 2), lax.rem(chip, 2)


class Links:
    def __init__(self, send, recv):
        self.send, self.recv = send, recv
        self.pos, self.core = position()
        self.ids, self.started = {}, []

    def at(self, axis, delta):
        return lax.rem(self.pos[axis] + delta, RING)

    def device(self, axis=None, delta=0):
        place = list(self.pos)
        core = self.core
        if axis is None:
            core = 1 - core
        else:
            place[axis] = self.at(axis, delta)
        return (place[0] * RING + place[1], place[2] * 2 + core)

    def copy(self, key, src, dst, device):
        index = self.ids.setdefault(key, len(self.ids))
        return pltpu.make_async_remote_copy(
            src_ref=src,
            dst_ref=dst,
            send_sem=self.send.at[index],
            recv_sem=self.recv.at[index],
            device_id=device,
            device_id_type=MESH,
        )

    def start(self, key, src, dst, device):
        copy = self.copy(key, src, dst, device)
        copy.start()
        self.started.append(copy)

    def wait(self, key, dst):
        self.copy(key, dst, dst, self.device()).wait_recv()

    def finish(self):
        for copy in self.started:
            copy.wait_send()
        self.started = []


class Gather(Links):
    def __init__(self, waves, send, recv, whole):
        super().__init__(send, recv)
        self.waves, self.whole = waves, whole

    def view(self, w, t, axes, core=None):
        first, rows = ROWS[w][t]
        index = [axes.get(axis, self.pos[axis]) for axis in range(3)]
        core = self.core if core is None else core
        return self.waves[w].at[index[0], index[1], index[2], core, pl.ds(first, rows), :]

    def push(self, key, view, device):
        self.start(key, view, view, device)

    def line(self, t, second=None, third=None, half=ALL):
        axes = {ORDER[t][0]: half}
        if second is not None:
            axes[ORDER[t][1]] = second
        if third is not None:
            axes[ORDER[t][2]] = third
        return axes

    def seconds(self, t):
        return [self.at(ORDER[t][1], delta) for delta in (0, 3, 1, 2)]

    def first_start(self, w, t):
        for delta in (1, 3, 2):
            self.push((w, t, 1, delta), self.view(w, t, {}), self.device(ORDER[t][0], delta))

    def third_line(self, w, t, j):
        view = self.view(w, t, self.line(t, self.seconds(t)[j]))
        for delta in (1, 3):
            self.push((w, t, 3, delta, j), view, self.device(ORDER[t][2], delta))
        self.sibling(w, t, j, 0)

    def shared(self, w, t, j, away):
        if self.whole[w][(0, 1, 2, 1)[away]]:
            return self.line(t, ALL, self.at(ORDER[t][2], 4 - away)) if j == 3 else None
        return self.line(t, self.seconds(t)[j], self.at(ORDER[t][2], 4 - away))

    def sibling(self, w, t, j, away):
        axes = self.shared(w, t, j, away)
        if axes is not None:
            self.push((w, t, "s", j, away), self.view(w, t, axes), self.device())

    def sibling_end(self, w, t, away):
        for j in range(4):
            axes = self.shared(w, t, j, away)
            if axes is not None:
                self.wait((w, t, "s", j, away), self.view(w, t, axes, core=1 - self.core))

    def first_end(self, w, t):
        axis = ORDER[t][0]
        for delta in (1, 3, 2):
            self.wait((w, t, 1, delta), self.view(w, t, {axis: self.at(axis, 4 - delta)}))
        view = self.view(w, t, self.line(t))
        for delta in (1, 3):
            self.push((w, t, 2, delta), view, self.device(ORDER[t][1], delta))
        self.third_line(w, t, 0)

    def second_pass(self, w, t, k):
        delta, half = HALVES[k]
        source = self.seconds(t)[k + 1]
        self.wait((w, t, 2, delta), self.view(w, t, self.line(t, source)))
        view = self.view(w, t, self.line(t, source, half=half))
        self.push((w, t, 2, delta, "f"), view, self.device(ORDER[t][1], delta))
        self.third_line(w, t, k + 1)

    def second_end(self, w, t):
        source = self.seconds(t)[3]
        for delta, half in HALVES:
            self.wait((w, t, 2, delta, "f"), self.view(w, t, self.line(t, source, half=half)))
        self.third_line(w, t, 3)

    def third_pass(self, w, t, j):
        axis, source = ORDER[t][2], self.seconds(t)[j]
        for delta, half in HALVES:
            origin = self.at(axis, 4 - delta)
            self.wait((w, t, 3, delta, j), self.view(w, t, self.line(t, source, origin)))
            view = self.view(w, t, self.line(t, source, origin, half=half))
            self.push((w, t, 3, delta, j, "f"), view, self.device(axis, delta))
            self.sibling(w, t, j, delta)

    def third_end(self, w, t, j):
        axis, source = ORDER[t][2], self.seconds(t)[j]
        for delta, half in HALVES:
            view = self.view(w, t, self.line(t, source, self.at(axis, 2), half=half))
            self.wait((w, t, 3, delta, j, "f"), view)
        self.sibling(w, t, j, 2)

    def take(self, name, w, *more):
        step = {
            "first": self.first_start,
            "line": self.first_end,
            "plane": self.second_pass,
            "planed": self.second_end,
            "pass": self.third_pass,
            "far": self.third_end,
            "share": self.sibling_end,
        }[name]
        for t in range(3):
            step(w, t, *more)


class Sum(Links):
    def __init__(self, sibling_half, stages, total, send, recv):
        super().__init__(send, recv)
        self.sibling_half, self.stages, self.total = sibling_half, stages, total
        self.half = K // 2

    def rows(self, core):
        return pl.ds(pl.multiple_of(core * self.half, self.half), self.half)

    def begin(self, matrix):
        self.matrix = matrix
        self.start("s", matrix.at[self.rows(1 - self.core)], self.sibling_half, self.device())

    def stage_start(self, stage, value):
        for t in range(3):
            first, rows = GRAM_ROWS[t]
            axis = ORDER[t][stage]
            own = self.stages.at[stage, self.pos[axis], pl.ds(first, rows)]
            own[...] = value[first : first + rows]
            for delta in (2, 1, 3):
                self.push((stage, t, delta), own, self.device(axis, delta))

    def push(self, key, view, device):
        self.start(key, view, view, device)

    def stage_end(self, stage):
        parts = []
        for t in range(3):
            first, rows = GRAM_ROWS[t]
            axis = ORDER[t][stage]
            for delta in (1, 3, 2):
                view = self.stages.at[stage, self.at(axis, 4 - delta), pl.ds(first, rows)]
                self.wait((stage, t, delta), view)
            slots = [self.stages[stage, p, first : first + rows] for p in range(RING)]
            parts.append((slots[0] + slots[1]) + (slots[2] + slots[3]))
        return jnp.concatenate(parts, axis=0)

    def take(self, step):
        (self.step_one, self.step_two, self.step_three, self.step_four, self.step_five)[step]()

    def step_one(self):
        self.wait("s", self.sibling_half)
        self.stage_start(0, self.matrix[self.rows(self.core)] + self.sibling_half[...])

    def step_two(self):
        self.stage_start(1, self.stage_end(0))

    def step_three(self):
        self.stage_start(2, self.stage_end(1))

    def step_four(self):
        mine = self.total.at[self.rows(self.core)]
        mine[...] = self.stage_end(2)
        self.start("e", mine, mine, self.device())

    def step_five(self):
        self.wait("e", self.total.at[self.rows(1 - self.core)])


def product(left, right, left_dim, right_dim):
    dims = (((left_dim,), (right_dim,)), ((), ()))
    return lax.dot_general(left, right, dims, precision=HIGHEST, preferred_element_type=jnp.float32)


def factor_inverse(matrix, result, panel=32, pivots=8):
    ids = [lax.broadcasted_iota(jnp.int32, (K, K), dim) for dim in (0, 1)]
    side = jnp.where(ids[0] == ids[1], 1.0, 0.0)
    row = lax.broadcasted_iota(jnp.int32, (panel, K), 0)
    lane = lax.broadcasted_iota(jnp.int32, (panel, K), 1)
    uppers, inverses = [], []
    for first in range(0, K, panel):
        a, w = matrix[:panel], side[:panel]
        for j in range(0, panel, pivots):
            span = range(pivots)
            cols = [
                jnp.broadcast_to(a[:, first + j + q : first + j + q + 1], (panel, K)) for q in span
            ]
            row_a = [a[j + q : j + q + 1] for q in span]
            row_w = [w[j + q : j + q + 1] for q in span]
            small = [[cols[k][j + q : j + q + 1] for k in span] for q in span]
            for q in span:
                inverse = 1.0 / small[q][q]
                ratio = {k: small[q][k] * inverse for k in range(q + 1, pivots)}
                for k in range(q + 1, pivots):
                    for m in range(k, pivots):
                        small[k][m] = small[k][m] - ratio[k] * small[q][m]
                    row_a[k] = row_a[k] - ratio[k] * row_a[q]
                    row_w[k] = row_w[k] - ratio[k] * row_w[q]
                weight = jnp.where(row > j + q, cols[q], 0.0) * inverse
                for k in range(q + 1, pivots):
                    cols[k] = cols[k] - cols[q] * ratio[k]
                a = a - weight * row_a[q]
                w = w - weight * row_w[q]
        diagonal = jnp.sum(jnp.where(lane == row + first, a, 0.0), axis=1, keepdims=True)
        scale = lax.rsqrt(diagonal)
        a = jnp.where(lane >= row + first, a * scale, 0.0)
        w = w * scale
        uppers.append(a)
        inverses.append(w)
        if first + panel < K:
            rest = a[:, first + panel :]
            matrix = matrix[panel:] - product(rest, a, 0, 0)
            side = side[panel:] - product(rest, w, 0, 0)
        yield
    result.extend((jnp.concatenate(uppers, axis=0), jnp.concatenate(inverses, axis=0)))


def kernel(
    cols_hbm,
    live_hbm,
    tiles_hbm,
    degree_hbm,
    basis_hbm,
    image_hbm,
    sum_hbm,
    cols,
    live,
    degree,
    basis,
    tiles,
    a0,
    a1,
    b0,
    b1,
    scale,
    total,
    gram,
    half_one,
    stages_one,
    sum_one,
    half_two,
    stages_two,
    sum_two,
    load_sem,
    send_a,
    recv_a,
    send_b,
    recv_b,
    send_g,
    recv_g,
    send_h,
    recv_h,
):
    items = float(BLK * 2 * RING**3)
    first = Gather((a0, a1), send_a, recv_a, WHOLE_ONE)
    second = Gather((b0, b1), send_b, recv_b, WHOLE_TWO)
    gram_one = Sum(half_one, stages_one, sum_one, send_g, recv_g)
    gram_two = Sum(half_two, stages_two, sum_two, send_h, recv_h)
    pos, core = first.pos, first.core

    barrier = pltpu.get_barrier_semaphore()
    near = [first.device()] + [first.device(axis, d) for axis in range(3) for d in (1, 2, 3)]
    for device in near:
        pl.semaphore_signal(barrier, inc=1, device_id=device, device_id_type=MESH)
    pairs = [(degree_hbm, degree), (basis_hbm, basis), (cols_hbm, cols), (live_hbm, live)]
    pairs += [(tiles_hbm.at[pl.ds(8 * i, 8)], tiles.at[pl.ds(8 * i, 8)]) for i in range(4)]
    loads = [pltpu.make_async_copy(*pair, load_sem.at[i]) for i, pair in enumerate(pairs)]
    for load in loads:
        load.start()

    def place(waves, w, value):
        waves[w][pos[0], pos[1], pos[2], core] = value.astype(jnp.bfloat16)

    loads[0].wait()
    for i in range(BLK // K):
        row_scale = 1.0 / jnp.sqrt(degree[pl.ds(i * K, K)].astype(jnp.float32))
        scale[pl.ds(i * K, K)] = jnp.broadcast_to(row_scale.reshape(1, K), (K, K)).T
    loads[1].wait()
    for w in range(WAVES):
        rows = pl.ds(w * DEPTH, DEPTH)
        place((a0, a1), w, scale[rows] * basis[rows].astype(jnp.float32))
    pl.semaphore_wait(barrier, len(near))

    def multiply(waves, w, groups, rows=pl.ds(0, BLK)):
        @pl.loop(*groups)
        def _(group):
            parts = []
            for u in range(GROUP):
                slot = group * GROUP + u
                col = cols[slot]
                picked = waves[w][
                    col // 32, lax.rem(col // 8, 4), lax.rem(col // 2, 4), lax.rem(col, 2)
                ]
                picked = jnp.where(slot < live[0], picked, jnp.zeros_like(picked))
                tile = tiles[slot, rows, pl.ds(w * DEPTH, DEPTH)]
                parts.append(jnp.dot(tile, picked, preferred_element_type=jnp.float32))
            while len(parts) > 1:
                parts = [left + right for left, right in zip(parts[::2], parts[1::2])]
            total[rows] += parts[0]

    total[...] = jnp.zeros_like(total)
    for name, *more in ROUND_ONE:
        if name == "multiply":
            multiply(first.waves, more[0], more[1:])
        elif name == "loaded":
            for load in loads[2:]:
                load.wait()
        else:
            first.take(name, *more)

    def half_image(w):
        rows = pl.ds(w * DEPTH, DEPTH)
        multiply(first.waves, 1, (0, SLOTS // GROUP), rows)
        image = total[rows] * scale[rows]
        total[rows] = image
        place((b0, b1), w, scale[rows] * image)

    factors = []
    half_image(0)
    for name, *more in ROUND_TWO:
        if name == "half":
            half_image(1)
        elif name == "gram":
            image = total[...]
            total[...] = jnp.zeros_like(total)
            gram[...] = product(image, image, 0, 0) * (1.0 / items)
            gram_one.begin(gram)
        elif name == "sum":
            gram_one.take(more[0])
        elif name == "eliminate":
            if more[0] == 0:
                elimination = factor_inverse(sum_one[...], factors)
            next(elimination)
        elif name == "multiply":
            multiply(second.waves, more[0], more[1:])
        else:
            second.take(name, *more)
    next(elimination, None)
    raw = total[...] * scale[...]
    image = product(raw, factors[1], 1, 1)
    total[...] = image
    out = pltpu.make_async_copy(total, image_hbm, load_sem.at[0])
    out.start()
    gram_one.finish()
    gram[...] = product(image, image, 0, 0) * (1.0 / items)
    gram_two.begin(gram)
    for step in range(5):
        gram_two.take(step)
    out_sum = pltpu.make_async_copy(sum_two, sum_hbm, load_sem.at[1])
    out_sum.start()
    first.finish()
    second.finish()
    gram_two.finish()
    out.wait()
    out_sum.wait()


def finish(image, gram, leading, factor):
    factors = []
    for _ in factor_inverse(gram[...], factors):
        pass
    upper, inverse = factors
    factor[...] = upper.T
    leading[...] = product(image[...], inverse, 1, 1)


def local(tile_data, tile_col, live_count, degree, start_basis):
    vmem, anywhere = pl.BlockSpec(memory_space=pltpu.VMEM), pl.BlockSpec(memory_space=pl.ANY)
    wave = pltpu.VMEM((RING, RING, RING, 2, DEPTH, K), jnp.bfloat16)
    sums = [
        pltpu.VMEM((K // 2, K), jnp.float32),
        pltpu.VMEM((3, RING, K // 2, K), jnp.float32),
        pltpu.VMEM((K, K), jnp.float32),
    ]
    dma = pltpu.SemaphoreType.DMA
    rows = jax.ShapeDtypeStruct((BLK, K), jnp.float32)
    square = jax.ShapeDtypeStruct((K, K), jnp.float32)
    image, gram = pl.pallas_call(
        kernel,
        out_shape=(rows, square),
        in_specs=[anywhere] * 5,
        out_specs=(anywhere, anywhere),
        scratch_shapes=[
            pltpu.SMEM((SLOTS,), jnp.int32),
            pltpu.SMEM((1,), jnp.int32),
            pltpu.VMEM((BLK,), jnp.int32),
            pltpu.VMEM((BLK, K), jnp.bfloat16),
            pltpu.VMEM((SLOTS, BLK, BLK), jnp.bfloat16),
            *[wave] * 4,
            pltpu.VMEM((BLK, K), jnp.float32),
            pltpu.VMEM((BLK, K), jnp.float32),
            pltpu.VMEM((K, K), jnp.float32),
            *sums * 2,
            dma((8,)),
            *[dma((COPIES,))] * 4,
            *[dma((SUMS,))] * 4,
        ],
        compiler_params=pltpu.CompilerParams(
            collective_id=0, has_side_effects=True, vmem_limit_bytes=58 * 2**20
        ),
        name="two_rounds",
    )(tile_col, live_count, tile_data, degree, start_basis)
    return pl.pallas_call(
        finish,
        out_shape=(rows, square),
        in_specs=[vmem] * 2,
        out_specs=(vmem, vmem),
        name="finish",
    )(image, gram)


def solution(mesh):
    placed = (
        P(("hst", "chip"), None, None),
        P(("hst", "chip")),
        P(("hst", "chip")),
        P(("hst", "chip")),
        P(("hst", "chip"), None),
    )
    return jax.shard_map(
        local,
        mesh=mesh,
        in_specs=placed,
        out_specs=(P(("hst", "chip"), None), P()),
        check_vma=False,
    )
```

```python
import functools

import jax
import jax.numpy as jnp
from jax import lax
from jax.experimental import pallas as pl
from jax.experimental.pallas import tpu as pltpu
from jax.sharding import PartitionSpec as P

BLK = 512
K = 128
SLOTS = 32
RING = 4
WAVES = 2
DEPTH = BLK // WAVES
MESH = pl.DeviceIdType.MESH
HIGHEST = lax.Precision.HIGHEST
ALL = pl.ds(0, RING)
HALVES = ((1, pl.ds(0, 2)), (3, pl.ds(2, 2)))
ORDER = ((1, 0, 2), (0, 2, 1), (2, 1, 0))
ROWS = (((0, 96), (96, 80), (176, 80)), ((0, 80), (80, 80), (160, 96)))
GRAM_ROWS = ((0, 24), (24, 24), (48, 16))
SENDS = 8
RECEIPTS = 26
SUMS = 5
GROUP = 16
WHOLE_ONE = ((False, False, False), (False, False, False))
WHOLE_TWO = ((False, False, False), (False, False, False))
ROUND_ONE = (
    ("first", 0), ("first", 1), ("line", 0), ("line", 1), ("plane", 0, 0), ("plane", 0, 1),
    ("plane", 1, 0), ("plane", 1, 1), ("planed", 0), ("pass", 0, 0), ("pass", 0, 1), ("pass", 0, 2),
    ("pass", 0, 3), ("planed", 1), ("pass", 1, 0), ("far", 0, 0), ("far", 0, 1), ("far", 0, 2),
    ("pass", 1, 1), ("pass", 1, 2), ("far", 0, 3), ("pass", 1, 3), ("share", 0), ("loaded",),
    ("multiply", 0, 0, 1), ("far", 1, 0), ("far", 1, 1), ("multiply", 0, 1, 2), ("far", 1, 2),
    ("far", 1, 3), ("share", 1),
)
ROUND_TWO = (
    ("first", 0), ("half",), ("first", 1), ("line", 0), ("gram",), ("sum", 0), ("line", 1),
    ("sum", 1), ("plane", 0, 0), ("plane", 0, 1), ("sum", 2), ("plane", 1, 0), ("plane", 1, 1),
    ("planed", 0), ("sum", 3), ("pass", 0, 0), ("sum", 4), ("eliminate", 0), ("eliminate", 1),
    ("eliminate", 2), ("pass", 0, 1), ("pass", 0, 2), ("pass", 0, 3), ("planed", 1), ("pass", 1, 0),
    ("eliminate", 3), ("far", 0, 0), ("pass", 1, 1), ("far", 0, 1), ("far", 0, 2), ("far", 0, 3),
    ("pass", 1, 2), ("share", 0), ("pass", 1, 3), ("multiply", 0, 0, 1), ("far", 1, 0),
    ("far", 1, 1), ("multiply", 0, 1, 2), ("far", 1, 2), ("far", 1, 3), ("share", 1),
    ("multiply", 1, 0, 2),
)


def position():
    host, chip = lax.axis_index("hst"), lax.axis_index("chip")
    return (host // RING, lax.rem(host, RING), chip // 2), lax.rem(chip, 2)


class Links:
    def __init__(self, send, recv):
        self.send, self.recv = send, recv
        self.pos, self.core = position()
        self.send_ids, self.recv_ids = {}, {}

    def at(self, axis, delta):
        return lax.rem(self.pos[axis] + delta, RING)

    def device(self, axis=None, delta=0):
        place = list(self.pos)
        core = self.core
        if axis is None:
            core = 1 - core
        else:
            place[axis] = self.at(axis, delta)
        return (place[0] * RING + place[1], place[2] * 2 + core)

    def copy(self, out, into, src, dst, device):
        return pltpu.make_async_remote_copy(
            src_ref=src,
            dst_ref=dst,
            send_sem=self.send.at[self.send_ids.setdefault(out, len(self.send_ids))],
            recv_sem=self.recv.at[self.recv_ids.setdefault(into, len(self.recv_ids))],
            device_id=device,
            device_id_type=MESH,
        )

    def wait(self, into, like):
        self.copy(next(iter(self.send_ids)), into, like, like, self.device()).wait_recv()

    def wait_sent(self, out, like):
        self.copy(out, next(iter(self.recv_ids)), like, like, self.device()).wait_send()


class Gather(Links):
    def __init__(self, waves, send, recv, whole):
        super().__init__(send, recv)
        self.waves, self.whole = waves, whole

    def view(self, w, t, axes):
        first, rows = ROWS[w][t]
        index = [axes.get(axis, self.pos[axis]) for axis in range(3)]
        return self.waves[w].at[index[0], index[1], index[2], self.core, pl.ds(first, rows), :]

    def blocks(self, w, y, x, z):
        return self.waves[w].at[pl.ds(0, y), pl.ds(0, x), pl.ds(0, z), 0]

    def push(self, out, into, w, t, axes, device):
        view = self.view(w, t, axes)
        self.copy((w, out), (w, into), view, view, device).start()

    def line(self, t, second=None, third=None, half=ALL):
        axes = {ORDER[t][0]: half}
        if second is not None:
            axes[ORDER[t][1]] = second
        if third is not None:
            axes[ORDER[t][2]] = third
        return axes

    def seconds(self, t):
        return [self.at(ORDER[t][1], delta) for delta in (0, 3, 1, 2)]

    def first_start(self, w):
        for t in range(3):
            for delta in (2, 1, 3):
                self.push("first", "first", w, t, {}, self.device(ORDER[t][0], delta))

    def third_line(self, w, t, j):
        axes = self.line(t, self.seconds(t)[j])
        for delta in (1, 3):
            self.push("third", ("third", j), w, t, axes, self.device(ORDER[t][2], delta))
        self.sibling(w, t, j, 0)

    def sibling(self, w, t, j, away):
        third = self.at(ORDER[t][2], 4 - away)
        if not self.whole[w][(0, 1, 2, 1)[away]]:
            self.push("share", "share", w, t, self.line(t, self.seconds(t)[j], third), self.device())
        elif j == 3:
            self.push("share", "share", w, t, self.line(t, ALL, third), self.device())

    def sibling_end(self, w):
        self.wait((w, "share"), self.blocks(w, 4, 4, 4))

    def first_end(self, w):
        self.wait((w, "first"), self.blocks(w, 1, 1, 3))
        for t in range(3):
            for delta in (1, 3):
                device = self.device(ORDER[t][1], delta)
                self.push("second", ("second", delta), w, t, self.line(t), device)
            self.third_line(w, t, 0)

    def second_pass(self, w, k):
        delta, half = HALVES[k]
        self.wait((w, ("second", delta)), self.blocks(w, 1, 1, 4))
        for t in range(3):
            axes = self.line(t, self.seconds(t)[k + 1], half=half)
            self.push("second", "halves", w, t, axes, self.device(ORDER[t][1], delta))
            self.third_line(w, t, k + 1)

    def second_end(self, w):
        self.wait((w, "halves"), self.blocks(w, 1, 1, 4))
        for t in range(3):
            self.third_line(w, t, 3)

    def third_pass(self, w, j):
        self.wait((w, ("third", j)), self.blocks(w, 1, 2, 4))
        for t in range(3):
            axis, source = ORDER[t][2], self.seconds(t)[j]
            for delta, half in HALVES:
                axes = self.line(t, source, self.at(axis, 4 - delta), half)
                self.push("third", ("far", j), w, t, axes, self.device(axis, delta))
                self.sibling(w, t, j, delta)

    def third_end(self, w, j):
        self.wait((w, ("far", j)), self.blocks(w, 1, 1, 4))
        for t in range(3):
            self.sibling(w, t, j, 2)

    def finish(self):
        for w in range(WAVES):
            self.wait_sent((w, "first"), self.blocks(w, 1, 1, 3))
            self.wait_sent((w, "second"), self.blocks(w, 1, 3, 4))
            self.wait_sent((w, "third"), self.blocks(w, 3, 4, 4))
            self.wait_sent((w, "share"), self.blocks(w, 4, 4, 4))

    def take(self, name, w, *more):
        step = {
            "first": self.first_start,
            "line": self.first_end,
            "plane": self.second_pass,
            "planed": self.second_end,
            "pass": self.third_pass,
            "far": self.third_end,
            "share": self.sibling_end,
        }[name]
        step(w, *more)


class Sum(Links):
    def __init__(self, sibling_half, stages, total, send, recv):
        super().__init__(send, recv)
        self.sibling_half, self.stages, self.total = sibling_half, stages, total
        self.half = K // 2

    def rows(self, core):
        return pl.ds(pl.multiple_of(core * self.half, self.half), self.half)

    def begin(self, matrix):
        self.matrix = matrix
        out = matrix.at[self.rows(1 - self.core)]
        self.copy("in", "in", out, self.sibling_half, self.device()).start()

    def stage_start(self, stage, value):
        for t in range(3):
            first, rows = GRAM_ROWS[t]
            axis = ORDER[t][stage]
            own = self.stages.at[stage, self.pos[axis], pl.ds(first, rows)]
            own[...] = value[first : first + rows]
            for delta in (2, 1, 3):
                self.copy(stage, stage, own, own, self.device(axis, delta)).start()

    def stage_end(self, stage):
        self.wait(stage, self.stages.at[stage, pl.ds(0, 3)])
        slots = [self.stages[stage, p] for p in range(RING)]
        return (slots[0] + slots[1]) + (slots[2] + slots[3])

    def take(self, step):
        if step == 0:
            self.wait("in", self.sibling_half)
            self.stage_start(0, self.matrix[self.rows(self.core)] + self.sibling_half[...])
        elif step < 3:
            self.stage_start(step, self.stage_end(step - 1))
        elif step == 3:
            mine = self.total.at[self.rows(self.core)]
            mine[...] = self.stage_end(2)
            self.copy("out", "out", mine, mine, self.device()).start()
        else:
            self.wait("out", self.total.at[self.rows(1 - self.core)])

    def finish(self):
        for stage in range(3):
            self.wait_sent(stage, self.stages.at[stage, pl.ds(0, 3)])
        self.wait_sent("in", self.sibling_half)
        self.wait_sent("out", self.total.at[self.rows(self.core)])


def product(left, right, left_dim, right_dim):
    dims = (((left_dim,), (right_dim,)), ((), ()))
    return lax.dot_general(left, right, dims, precision=HIGHEST, preferred_element_type=jnp.float32)


def factor_inverse(matrix, result, panel=32, pivots=8):
    ids = [lax.broadcasted_iota(jnp.int32, (K, K), dim) for dim in (0, 1)]
    side = jnp.where(ids[0] == ids[1], 1.0, 0.0)
    row = lax.broadcasted_iota(jnp.int32, (panel, K), 0)
    lane = lax.broadcasted_iota(jnp.int32, (panel, K), 1)
    uppers, inverses = [], []
    for first in range(0, K, panel):
        a, w = matrix[:panel], side[:panel]
        for j in range(0, panel, pivots):
            span = range(pivots)
            cols = [
                jnp.broadcast_to(a[:, first + j + q : first + j + q + 1], (panel, K)) for q in span
            ]
            row_a = [a[j + q : j + q + 1] for q in span]
            row_w = [w[j + q : j + q + 1] for q in span]
            small = [[cols[k][j + q : j + q + 1] for k in span] for q in span]
            for q in span:
                inverse = 1.0 / small[q][q]
                ratio = {k: small[q][k] * inverse for k in range(q + 1, pivots)}
                for k in range(q + 1, pivots):
                    for m in range(k, pivots):
                        small[k][m] = small[k][m] - ratio[k] * small[q][m]
                    row_a[k] = row_a[k] - ratio[k] * row_a[q]
                    row_w[k] = row_w[k] - ratio[k] * row_w[q]
                weight = jnp.where(row > j + q, cols[q], 0.0) * inverse
                for k in range(q + 1, pivots):
                    cols[k] = cols[k] - cols[q] * ratio[k]
                a = a - weight * row_a[q]
                w = w - weight * row_w[q]
        diagonal = jnp.sum(jnp.where(lane == row + first, a, 0.0), axis=1, keepdims=True)
        scale = lax.rsqrt(diagonal)
        a = jnp.where(lane >= row + first, a * scale, 0.0)
        w = w * scale
        uppers.append(a)
        inverses.append(w)
        if first + panel < K:
            rest = a[:, first + panel :]
            matrix = matrix[panel:] - product(rest, a, 0, 0)
            side = side[panel:] - product(rest, w, 0, 0)
        yield
    result.extend((jnp.concatenate(uppers, axis=0), jnp.concatenate(inverses, axis=0)))


def kernel(
    cols_hbm,
    live_hbm,
    tiles_hbm,
    degree_hbm,
    basis_hbm,
    image_hbm,
    sum_hbm,
    cols,
    live,
    degree,
    basis,
    tiles,
    a0,
    a1,
    b0,
    b1,
    scale,
    total,
    gram,
    half_one,
    stages_one,
    sum_one,
    half_two,
    stages_two,
    sum_two,
    load_sem,
    send_a,
    recv_a,
    send_b,
    recv_b,
    send_g,
    recv_g,
    send_h,
    recv_h,
):
    items = float(BLK * 2 * RING**3)
    first = Gather((a0, a1), send_a, recv_a, WHOLE_ONE)
    second = Gather((b0, b1), send_b, recv_b, WHOLE_TWO)
    gram_one = Sum(half_one, stages_one, sum_one, send_g, recv_g)
    gram_two = Sum(half_two, stages_two, sum_two, send_h, recv_h)
    pos, core = first.pos, first.core

    barrier = pltpu.get_barrier_semaphore()
    near = [first.device()] + [first.device(axis, d) for axis in range(3) for d in (1, 2, 3)]
    for device in near:
        pl.semaphore_signal(barrier, inc=1, device_id=device, device_id_type=MESH)
    pairs = [(degree_hbm, degree), (basis_hbm, basis), (cols_hbm, cols), (live_hbm, live)]
    pairs += [(tiles_hbm.at[pl.ds(8 * i, 8)], tiles.at[pl.ds(8 * i, 8)]) for i in range(4)]
    loads = [pltpu.make_async_copy(*pair, load_sem.at[i]) for i, pair in enumerate(pairs)]
    for load in loads:
        load.start()

    def place(waves, w, value):
        waves[w][pos[0], pos[1], pos[2], core] = value.astype(jnp.bfloat16)

    loads[0].wait()
    for i in range(BLK // K):
        row_scale = 1.0 / jnp.sqrt(degree[pl.ds(i * K, K)].astype(jnp.float32))
        scale[pl.ds(i * K, K)] = jnp.broadcast_to(row_scale.reshape(1, K), (K, K)).T
    loads[1].wait()
    for w in range(WAVES):
        rows = pl.ds(w * DEPTH, DEPTH)
        place((a0, a1), w, scale[rows] * basis[rows].astype(jnp.float32))
    pl.semaphore_wait(barrier, len(near))

    def multiply(waves, w, groups, rows=pl.ds(0, BLK)):
        @pl.loop(*groups)
        def _(group):
            parts = []
            for u in range(GROUP):
                slot = group * GROUP + u
                col = cols[slot]
                picked = waves[w][
                    col // 32, lax.rem(col // 8, 4), lax.rem(col // 2, 4), lax.rem(col, 2)
                ]
                picked = jnp.where(slot < live[0], picked, jnp.zeros_like(picked))
                tile = tiles[slot, rows, pl.ds(w * DEPTH, DEPTH)]
                parts.append(jnp.dot(tile, picked, preferred_element_type=jnp.float32))
            while len(parts) > 1:
                parts = [left + right for left, right in zip(parts[::2], parts[1::2])]
            total[rows] += parts[0]

    total[...] = jnp.zeros_like(total)
    for name, *more in ROUND_ONE:
        if name == "multiply":
            multiply(first.waves, more[0], more[1:])
        elif name == "loaded":
            for load in loads[2:]:
                load.wait()
        else:
            first.take(name, *more)

    def half_image(w):
        rows = pl.ds(w * DEPTH, DEPTH)
        multiply(first.waves, 1, (0, SLOTS // GROUP), rows)
        image = total[rows] * scale[rows]
        total[rows] = image
        place((b0, b1), w, scale[rows] * image)

    factors = []
    half_image(0)
    for name, *more in ROUND_TWO:
        if name == "half":
            half_image(1)
        elif name == "gram":
            image = total[...]
            total[...] = jnp.zeros_like(total)
            gram[...] = product(image, image, 0, 0) * (1.0 / items)
            gram_one.begin(gram)
        elif name == "sum":
            gram_one.take(more[0])
        elif name == "eliminate":
            if more[0] == 0:
                elimination = factor_inverse(sum_one[...], factors)
            next(elimination)
        elif name == "multiply":
            multiply(second.waves, more[0], more[1:])
        else:
            second.take(name, *more)
    next(elimination, None)
    raw = total[...] * scale[...]
    image = product(raw, factors[1], 1, 1)
    total[...] = image
    out = pltpu.make_async_copy(total, image_hbm, load_sem.at[0])
    out.start()
    gram_one.finish()
    gram[...] = product(image, image, 0, 0) * (1.0 / items)
    gram_two.begin(gram)
    for step in range(5):
        gram_two.take(step)
    out_sum = pltpu.make_async_copy(sum_two, sum_hbm, load_sem.at[1])
    out_sum.start()
    first.finish()
    second.finish()
    gram_two.finish()
    out.wait()
    out_sum.wait()


def finish(image, gram, leading, factor):
    factors = []
    for _ in factor_inverse(gram[...], factors):
        pass
    upper, inverse = factors
    factor[...] = upper.T
    leading[...] = product(image[...], inverse, 1, 1)


def local(tile_data, tile_col, live_count, degree, start_basis):
    vmem, anywhere = pl.BlockSpec(memory_space=pltpu.VMEM), pl.BlockSpec(memory_space=pl.ANY)
    wave = pltpu.VMEM((RING, RING, RING, 2, DEPTH, K), jnp.bfloat16)
    sums = [
        pltpu.VMEM((K // 2, K), jnp.float32),
        pltpu.VMEM((3, RING, K // 2, K), jnp.float32),
        pltpu.VMEM((K, K), jnp.float32),
    ]
    dma = pltpu.SemaphoreType.DMA
    rows = jax.ShapeDtypeStruct((BLK, K), jnp.float32)
    square = jax.ShapeDtypeStruct((K, K), jnp.float32)
    image, gram = pl.pallas_call(
        kernel,
        out_shape=(rows, square),
        in_specs=[anywhere] * 5,
        out_specs=(anywhere, anywhere),
        scratch_shapes=[
            pltpu.SMEM((SLOTS,), jnp.int32),
            pltpu.SMEM((1,), jnp.int32),
            pltpu.VMEM((BLK,), jnp.int32),
            pltpu.VMEM((BLK, K), jnp.bfloat16),
            pltpu.VMEM((SLOTS, BLK, BLK), jnp.bfloat16),
            *[wave] * 4,
            pltpu.VMEM((BLK, K), jnp.float32),
            pltpu.VMEM((BLK, K), jnp.float32),
            pltpu.VMEM((K, K), jnp.float32),
            *sums * 2,
            dma((8,)),
            *[dma((SENDS,)), dma((RECEIPTS,))] * 2,
            *[dma((SUMS,))] * 4,
        ],
        compiler_params=pltpu.CompilerParams(
            collective_id=0, has_side_effects=True, vmem_limit_bytes=58 * 2**20
        ),
        name="two_rounds",
    )(tile_col, live_count, tile_data, degree, start_basis)
    return pl.pallas_call(
        finish,
        out_shape=(rows, square),
        in_specs=[vmem] * 2,
        out_specs=(vmem, vmem),
        name="finish",
    )(image, gram)


def solution(mesh):
    placed = (
        P(("hst", "chip"), None, None),
        P(("hst", "chip")),
        P(("hst", "chip")),
        P(("hst", "chip")),
        P(("hst", "chip"), None),
    )
    return jax.shard_map(
        local,
        mesh=mesh,
        in_specs=placed,
        out_specs=(P(("hst", "chip"), None), P()),
        check_vma=False,
    )
```

```python
import functools

import jax
import jax.numpy as jnp
from jax import lax
from jax.experimental import pallas as pl
from jax.experimental.pallas import tpu as pltpu
from jax.sharding import PartitionSpec as P

BLK = 512
K = 128
SLOTS = 32
RING = 4
WAVES = 2
DEPTH = BLK // WAVES
MESH = pl.DeviceIdType.MESH
HIGHEST = lax.Precision.HIGHEST
ALL = pl.ds(0, RING)
HALVES = ((1, pl.ds(0, 2)), (3, pl.ds(2, 2)))
ORDER = ((1, 0, 2), (0, 2, 1), (2, 1, 0))
ROWS = (((0, 96), (96, 80), (176, 80)), ((0, 80), (80, 80), (160, 96)))
GRAM_ROWS = ((0, 24), (24, 24), (48, 16))
SENDS = 8
RECEIPTS = 28
SUMS = 5
GROUP = 16
ROUND_ONE = (
    ("first", 0), ("first", 1), ("line", 0), ("line", 1), ("plane", 0, 0), ("plane", 0, 1),
    ("plane", 1, 0), ("planed", 0), ("pass", 0, 0), ("plane", 1, 1), ("pass", 0, 1), ("pass", 0, 2),
    ("far", 0, 0), ("pass", 0, 3), ("planed", 1), ("pass", 1, 0), ("far", 0, 1), ("far", 0, 2),
    ("pass", 1, 1), ("far", 0, 3), ("pass", 1, 2), ("share", 0), ("pass", 1, 3), ("loaded",),
    ("multiply", 0, 0, 1), ("far", 1, 0), ("far", 1, 1), ("multiply", 0, 1, 2), ("far", 1, 2),
    ("far", 1, 3), ("share", 1),
)
ROUND_TWO = (
    ("first", 0), ("half",), ("first", 1), ("line", 0), ("gram",), ("line", 1), ("sum", 0),
    ("plane", 0, 0), ("plane", 0, 1), ("sum", 1), ("plane", 1, 0), ("plane", 1, 1), ("sum", 2),
    ("planed", 0), ("planed", 1), ("pass", 0, 0), ("pass", 0, 1), ("sum", 3), ("pass", 0, 2),
    ("sum", 4), ("eliminate", 0), ("pass", 0, 3), ("pass", 1, 0), ("eliminate", 1), ("pass", 1, 1),
    ("pass", 1, 2), ("pass", 1, 3), ("far", 0, 0), ("eliminate", 2), ("far", 0, 1), ("far", 0, 2),
    ("far", 0, 3), ("far", 1, 0), ("eliminate", 3), ("far", 1, 1), ("share", 0),
    ("multiply", 0, 0, 1), ("far", 1, 2), ("far", 1, 3), ("multiply", 0, 1, 2), ("share", 1),
    ("multiply", 1, 0, 2),
)


def position():
    host, chip = lax.axis_index("hst"), lax.axis_index("chip")
    return (host // RING, lax.rem(host, RING), chip // 2), lax.rem(chip, 2)


class Links:
    def __init__(self, send, recv):
        self.send, self.recv = send, recv
        self.pos, self.core = position()
        self.send_ids, self.recv_ids = {}, {}

    def at(self, axis, delta):
        return lax.rem(self.pos[axis] + delta, RING)

    def device(self, axis=None, delta=0):
        place = list(self.pos)
        core = self.core
        if axis is None:
            core = 1 - core
        else:
            place[axis] = self.at(axis, delta)
        return (place[0] * RING + place[1], place[2] * 2 + core)

    def copy(self, out, into, src, dst, device):
        return pltpu.make_async_remote_copy(
            src_ref=src,
            dst_ref=dst,
            send_sem=self.send.at[self.send_ids.setdefault(out, len(self.send_ids))],
            recv_sem=self.recv.at[self.recv_ids.setdefault(into, len(self.recv_ids))],
            device_id=device,
            device_id_type=MESH,
        )

    def wait(self, into, like):
        self.copy(next(iter(self.send_ids)), into, like, like, self.device()).wait_recv()

    def wait_sent(self, out, like):
        self.copy(out, next(iter(self.recv_ids)), like, like, self.device()).wait_send()


class Gather(Links):
    def __init__(self, waves, send, recv):
        super().__init__(send, recv)
        self.waves = waves

    def view(self, w, t, axes):
        first, rows = ROWS[w][t]
        index = [axes.get(axis, self.pos[axis]) for axis in range(3)]
        return self.waves[w].at[index[0], index[1], index[2], self.core, pl.ds(first, rows), :]

    def blocks(self, w, y, x, z):
        return self.waves[w].at[pl.ds(0, y), pl.ds(0, x), pl.ds(0, z), 0]

    def push(self, out, into, w, t, axes, device):
        view = self.view(w, t, axes)
        self.copy((w, out), (w, into), view, view, device).start()

    def line(self, t, second=None, third=None, half=ALL):
        axes = {ORDER[t][0]: half}
        if second is not None:
            axes[ORDER[t][1]] = second
        if third is not None:
            axes[ORDER[t][2]] = third
        return axes

    def seconds(self, t):
        return [self.at(ORDER[t][1], delta) for delta in (0, 3, 1, 2)]

    def first_start(self, w):
        for t in range(3):
            for delta in (2, 1, 3):
                into = "opposite" if delta == 2 else "first"
                self.push("first", into, w, t, {}, self.device(ORDER[t][0], delta))
        self.block(w, {})

    def block(self, w, *blocks):
        for step in (1, 2):
            for t in range(3):
                for delta in (1, 3):
                    into = ("second", delta) if step == 1 else ("third", 0)
                    device = self.device(ORDER[t][step], delta)
                    for axes in blocks:
                        out = "second" if step == 1 else "third"
                        self.push(out, into, w, t, axes if axes == {} else axes[t], device)

    def third_line(self, w, t, j):
        axes = self.line(t, self.seconds(t)[j])
        for delta in (1, 3):
            self.push("third", ("third", j), w, t, axes, self.device(ORDER[t][2], delta))
        self.sibling(w, t, j, 0)

    def sibling(self, w, t, j, away):
        axes = self.line(t, self.seconds(t)[j], self.at(ORDER[t][2], 4 - away))
        self.push("share", "share", w, t, axes, self.device())

    def sibling_end(self, w):
        self.wait((w, "share"), self.blocks(w, 4, 4, 4))

    def first_end(self, w):
        from_start = [
            [{ORDER[t][0]: self.at(ORDER[t][0], delta)} for t in range(3)] for delta in (3, 1, 2)
        ]
        self.wait((w, "first"), self.blocks(w, 1, 1, 2))
        self.block(w, *from_start[:2])
        self.wait((w, "opposite"), self.blocks(w, 1, 1, 1))
        self.block(w, from_start[2])
        for t in range(3):
            self.sibling(w, t, 0, 0)

    def second_pass(self, w, k):
        delta, half = HALVES[k]
        self.wait((w, ("second", delta)), self.blocks(w, 1, 1, 4))
        for t in range(3):
            axes = self.line(t, self.seconds(t)[k + 1], half=half)
            self.push("second", "halves", w, t, axes, self.device(ORDER[t][1], delta))
        for t in range(3):
            self.third_line(w, t, k + 1)

    def second_end(self, w):
        self.wait((w, "halves"), self.blocks(w, 1, 1, 4))
        for t in range(3):
            self.third_line(w, t, 3)

    def third_pass(self, w, j):
        self.wait((w, ("third", j)), self.blocks(w, 1, 2, 4))
        for t in range(3):
            axis, source = ORDER[t][2], self.seconds(t)[j]
            for delta, half in HALVES:
                axes = self.line(t, source, self.at(axis, 4 - delta), half)
                self.push("third", ("far", j), w, t, axes, self.device(axis, delta))
        for t in range(3):
            for delta in (1, 3):
                self.sibling(w, t, j, delta)

    def third_end(self, w, j):
        self.wait((w, ("far", j)), self.blocks(w, 1, 1, 4))
        for t in range(3):
            self.sibling(w, t, j, 2)

    def finish(self):
        for w in range(WAVES):
            self.wait_sent((w, "first"), self.blocks(w, 1, 1, 3))
            self.wait_sent((w, "second"), self.blocks(w, 1, 3, 4))
            self.wait_sent((w, "third"), self.blocks(w, 3, 4, 4))
            self.wait_sent((w, "share"), self.blocks(w, 4, 4, 4))

    def take(self, name, w, *more):
        step = {
            "first": self.first_start,
            "line": self.first_end,
            "plane": self.second_pass,
            "planed": self.second_end,
            "pass": self.third_pass,
            "far": self.third_end,
            "share": self.sibling_end,
        }[name]
        step(w, *more)


class Sum(Links):
    def __init__(self, sibling_half, stages, total, send, recv):
        super().__init__(send, recv)
        self.sibling_half, self.stages, self.total = sibling_half, stages, total
        self.half = K // 2

    def rows(self, core):
        return pl.ds(pl.multiple_of(core * self.half, self.half), self.half)

    def begin(self, matrix):
        self.matrix = matrix
        out = matrix.at[self.rows(1 - self.core)]
        self.copy("in", "in", out, self.sibling_half, self.device()).start()

    def stage_start(self, stage, value):
        parts = []
        for t in range(3):
            first, rows = GRAM_ROWS[t]
            axis = ORDER[t][stage]
            own = self.stages.at[stage, self.pos[axis], pl.ds(first, rows)]
            own[...] = value[first : first + rows]
            parts.append((axis, own))
        for delta in (2, 1, 3):
            for axis, own in parts:
                self.copy(stage, stage, own, own, self.device(axis, delta)).start()

    def stage_end(self, stage):
        self.wait(stage, self.stages.at[stage, pl.ds(0, 3)])
        slots = [self.stages[stage, p] for p in range(RING)]
        return (slots[0] + slots[1]) + (slots[2] + slots[3])

    def take(self, step):
        if step == 0:
            self.wait("in", self.sibling_half)
            self.stage_start(0, self.matrix[self.rows(self.core)] + self.sibling_half[...])
        elif step < 3:
            self.stage_start(step, self.stage_end(step - 1))
        elif step == 3:
            mine = self.total.at[self.rows(self.core)]
            mine[...] = self.stage_end(2)
            self.copy("out", "out", mine, mine, self.device()).start()
        else:
            self.wait("out", self.total.at[self.rows(1 - self.core)])

    def finish(self):
        for stage in range(3):
            self.wait_sent(stage, self.stages.at[stage, pl.ds(0, 3)])
        self.wait_sent("in", self.sibling_half)
        self.wait_sent("out", self.total.at[self.rows(self.core)])


def product(left, right, left_dim, right_dim):
    dims = (((left_dim,), (right_dim,)), ((), ()))
    return lax.dot_general(left, right, dims, precision=HIGHEST, preferred_element_type=jnp.float32)


def factor_inverse(matrix, result, panel=32, pivots=8):
    ids = [lax.broadcasted_iota(jnp.int32, (K, K), dim) for dim in (0, 1)]
    side = jnp.where(ids[0] == ids[1], 1.0, 0.0)
    row = lax.broadcasted_iota(jnp.int32, (panel, K), 0)
    lane = lax.broadcasted_iota(jnp.int32, (panel, K), 1)
    uppers, inverses = [], []
    for first in range(0, K, panel):
        a, w = matrix[:panel], side[:panel]
        for j in range(0, panel, pivots):
            span = range(pivots)
            cols = [
                jnp.broadcast_to(a[:, first + j + q : first + j + q + 1], (panel, K)) for q in span
            ]
            row_a = [a[j + q : j + q + 1] for q in span]
            row_w = [w[j + q : j + q + 1] for q in span]
            small = [[cols[k][j + q : j + q + 1] for k in span] for q in span]
            for q in span:
                inverse = 1.0 / small[q][q]
                ratio = {k: small[q][k] * inverse for k in range(q + 1, pivots)}
                for k in range(q + 1, pivots):
                    for m in range(k, pivots):
                        small[k][m] = small[k][m] - ratio[k] * small[q][m]
                    row_a[k] = row_a[k] - ratio[k] * row_a[q]
                    row_w[k] = row_w[k] - ratio[k] * row_w[q]
                weight = jnp.where(row > j + q, cols[q], 0.0) * inverse
                for k in range(q + 1, pivots):
                    cols[k] = cols[k] - cols[q] * ratio[k]
                a = a - weight * row_a[q]
                w = w - weight * row_w[q]
        diagonal = jnp.sum(jnp.where(lane == row + first, a, 0.0), axis=1, keepdims=True)
        scale = lax.rsqrt(diagonal)
        a = jnp.where(lane >= row + first, a * scale, 0.0)
        w = w * scale
        uppers.append(a)
        inverses.append(w)
        if first + panel < K:
            rest = a[:, first + panel :]
            matrix = matrix[panel:] - product(rest, a, 0, 0)
            side = side[panel:] - product(rest, w, 0, 0)
        yield
    result.extend((jnp.concatenate(uppers, axis=0), jnp.concatenate(inverses, axis=0)))


def kernel(
    cols_hbm,
    live_hbm,
    tiles_hbm,
    degree_hbm,
    basis_hbm,
    image_hbm,
    sum_hbm,
    cols,
    live,
    degree,
    basis,
    tiles,
    a0,
    a1,
    b0,
    b1,
    scale,
    total,
    gram,
    half_one,
    stages_one,
    sum_one,
    half_two,
    stages_two,
    sum_two,
    load_sem,
    send_a,
    recv_a,
    send_b,
    recv_b,
    send_g,
    recv_g,
    send_h,
    recv_h,
):
    items = float(BLK * 2 * RING**3)
    first = Gather((a0, a1), send_a, recv_a)
    second = Gather((b0, b1), send_b, recv_b)
    gram_one = Sum(half_one, stages_one, sum_one, send_g, recv_g)
    gram_two = Sum(half_two, stages_two, sum_two, send_h, recv_h)
    pos, core = first.pos, first.core

    barrier = pltpu.get_barrier_semaphore()
    near = [first.device()] + [first.device(axis, d) for axis in range(3) for d in (1, 2, 3)]
    for device in near:
        pl.semaphore_signal(barrier, inc=1, device_id=device, device_id_type=MESH)
    pairs = [(degree_hbm, degree), (basis_hbm, basis), (cols_hbm, cols), (live_hbm, live)]
    pairs += [(tiles_hbm.at[pl.ds(8 * i, 8)], tiles.at[pl.ds(8 * i, 8)]) for i in range(4)]
    loads = [pltpu.make_async_copy(*pair, load_sem.at[i]) for i, pair in enumerate(pairs)]
    for load in loads:
        load.start()

    def place(waves, w, value):
        waves[w][pos[0], pos[1], pos[2], core] = value.astype(jnp.bfloat16)

    loads[0].wait()
    for i in range(BLK // K):
        row_scale = 1.0 / jnp.sqrt(degree[pl.ds(i * K, K)].astype(jnp.float32))
        scale[pl.ds(i * K, K)] = jnp.broadcast_to(row_scale.reshape(1, K), (K, K)).T
    loads[1].wait()
    for w in range(WAVES):
        rows = pl.ds(w * DEPTH, DEPTH)
        place((a0, a1), w, scale[rows] * basis[rows].astype(jnp.float32))
    pl.semaphore_wait(barrier, len(near))

    def multiply(waves, w, groups, rows=pl.ds(0, BLK)):
        @pl.loop(*groups)
        def _(group):
            parts = []
            for u in range(GROUP):
                slot = group * GROUP + u
                col = cols[slot]
                picked = waves[w][
                    col // 32, lax.rem(col // 8, 4), lax.rem(col // 2, 4), lax.rem(col, 2)
                ]
                picked = jnp.where(slot < live[0], picked, jnp.zeros_like(picked))
                tile = tiles[slot, rows, pl.ds(w * DEPTH, DEPTH)]
                parts.append(jnp.dot(tile, picked, preferred_element_type=jnp.float32))
            while len(parts) > 1:
                parts = [left + right for left, right in zip(parts[::2], parts[1::2])]
            total[rows] += parts[0]

    total[...] = jnp.zeros_like(total)
    for name, *more in ROUND_ONE:
        if name == "multiply":
            multiply(first.waves, more[0], more[1:])
        elif name == "loaded":
            for load in loads[2:]:
                load.wait()
        else:
            first.take(name, *more)

    def half_image(w):
        rows = pl.ds(w * DEPTH, DEPTH)
        multiply(first.waves, 1, (0, SLOTS // GROUP), rows)
        image = total[rows] * scale[rows]
        total[rows] = image
        place((b0, b1), w, scale[rows] * image)

    factors = []
    half_image(0)
    for name, *more in ROUND_TWO:
        if name == "half":
            half_image(1)
        elif name == "gram":
            image = total[...]
            total[...] = jnp.zeros_like(total)
            gram[...] = product(image, image, 0, 0) * (1.0 / items)
            gram_one.begin(gram)
        elif name == "sum":
            gram_one.take(more[0])
        elif name == "eliminate":
            if more[0] == 0:
                elimination = factor_inverse(sum_one[...], factors)
            next(elimination)
        elif name == "multiply":
            multiply(second.waves, more[0], more[1:])
        else:
            second.take(name, *more)
    next(elimination, None)
    raw = total[...] * scale[...]
    image = product(raw, factors[1], 1, 1)
    total[...] = image
    out = pltpu.make_async_copy(total, image_hbm, load_sem.at[0])
    out.start()
    gram_one.finish()
    gram[...] = product(image, image, 0, 0) * (1.0 / items)
    gram_two.begin(gram)
    for step in range(5):
        gram_two.take(step)
    out_sum = pltpu.make_async_copy(sum_two, sum_hbm, load_sem.at[1])
    out_sum.start()
    first.finish()
    second.finish()
    gram_two.finish()
    out.wait()
    out_sum.wait()


def finish(image, gram, leading, factor):
    factors = []
    for _ in factor_inverse(gram[...], factors, panel=64):
        pass
    upper, inverse = factors
    factor[...] = upper.T
    leading[...] = product(image[...], inverse, 1, 1)


def local(tile_data, tile_col, live_count, degree, start_basis):
    vmem, anywhere = pl.BlockSpec(memory_space=pltpu.VMEM), pl.BlockSpec(memory_space=pl.ANY)
    wave = pltpu.VMEM((RING, RING, RING, 2, DEPTH, K), jnp.bfloat16)
    sums = [
        pltpu.VMEM((K // 2, K), jnp.float32),
        pltpu.VMEM((3, RING, K // 2, K), jnp.float32),
        pltpu.VMEM((K, K), jnp.float32),
    ]
    dma = pltpu.SemaphoreType.DMA
    rows = jax.ShapeDtypeStruct((BLK, K), jnp.float32)
    square = jax.ShapeDtypeStruct((K, K), jnp.float32)
    image, gram = pl.pallas_call(
        kernel,
        out_shape=(rows, square),
        in_specs=[anywhere] * 5,
        out_specs=(anywhere, anywhere),
        scratch_shapes=[
            pltpu.SMEM((SLOTS,), jnp.int32),
            pltpu.SMEM((1,), jnp.int32),
            pltpu.VMEM((BLK,), jnp.int32),
            pltpu.VMEM((BLK, K), jnp.bfloat16),
            pltpu.VMEM((SLOTS, BLK, BLK), jnp.bfloat16),
            *[wave] * 4,
            pltpu.VMEM((BLK, K), jnp.float32),
            pltpu.VMEM((BLK, K), jnp.float32),
            pltpu.VMEM((K, K), jnp.float32),
            *sums * 2,
            dma((8,)),
            *[dma((SENDS,)), dma((RECEIPTS,))] * 2,
            *[dma((SUMS,))] * 4,
        ],
        compiler_params=pltpu.CompilerParams(
            collective_id=0, has_side_effects=True, vmem_limit_bytes=58 * 2**20
        ),
        name="two_rounds",
    )(tile_col, live_count, tile_data, degree, start_basis)
    return pl.pallas_call(
        finish,
        out_shape=(rows, square),
        in_specs=[vmem] * 2,
        out_specs=(vmem, vmem),
        name="finish",
    )(image, gram)


def solution(mesh):
    placed = (
        P(("hst", "chip"), None, None),
        P(("hst", "chip")),
        P(("hst", "chip")),
        P(("hst", "chip")),
        P(("hst", "chip"), None),
    )
    return jax.shard_map(
        local,
        mesh=mesh,
        in_specs=placed,
        out_specs=(P(("hst", "chip"), None), P()),
        check_vma=False,
    )
```

```python
import functools

import jax
import jax.numpy as jnp
from jax import lax
from jax.experimental import pallas as pl
from jax.experimental.pallas import tpu as pltpu
from jax.sharding import PartitionSpec as P

BLK = 512
K = 128
SLOTS = 32
RING = 4
WAVES = 4
DEPTH = BLK // WAVES
MESH = pl.DeviceIdType.MESH
HIGHEST = lax.Precision.HIGHEST
ALL = pl.ds(0, RING)
HALVES = ((1, pl.ds(0, 2)), (3, pl.ds(2, 2)))
ORDER = ((1, 0, 2), (0, 2, 1), (2, 1, 0))
ROWS = (
    ((0, 48), (48, 48), (96, 32)),
    ((0, 32), (32, 48), (80, 48)),
    ((0, 48), (48, 32), (80, 48)),
    ((0, 48), (48, 48), (96, 32)),
)
GRAM_ROWS = ((0, 24), (24, 24), (48, 16))
SENDS = 4
RECEIPTS = 56
SUMS = 5
GROUP = 16
WHOLE = (0, 1, 2)
EARLY = (0, 1)
ROUND_ONE = (
    ("first", 0), ("first", 2), ("first", 1), ("first", 3), ("line", 0), ("line", 1), ("line", 2),
    ("plane", 0, 0), ("plane", 0, 1), ("plane", 2, 0), ("plane", 1, 0), ("plane", 1, 1),
    ("planed", 0), ("pass", 0, 0), ("plane", 2, 1), ("planed", 1), ("pass", 0, 1), ("line", 3),
    ("pass", 0, 2), ("pass", 1, 0), ("pass", 0, 3), ("planed", 2), ("far", 0, 0), ("plane", 3, 0),
    ("plane", 3, 1), ("pass", 2, 0), ("far", 0, 1), ("far", 1, 0), ("far", 0, 2), ("pass", 1, 1),
    ("far", 0, 3), ("pass", 1, 2), ("pass", 1, 3), ("pass", 2, 1), ("share", 0), ("loaded",),
    ("multiply", 0, 0, 1), ("planed", 3), ("pass", 2, 2), ("pass", 2, 3), ("multiply", 0, 1, 2),
    ("far", 1, 1), ("far", 1, 2), ("pass", 3, 0), ("far", 1, 3), ("pass", 3, 1), ("far", 2, 0),
    ("pass", 3, 2), ("far", 2, 1), ("pass", 3, 3), ("share", 1), ("multiply", 1, 0, 1),
    ("far", 2, 2), ("far", 2, 3), ("multiply", 1, 1, 2), ("far", 3, 0), ("far", 3, 1), ("share", 2),
    ("multiply", 2, 0, 1), ("far", 3, 2), ("far", 3, 3), ("multiply", 2, 1, 2), ("share", 3),
)
ROUND_TWO = (
    ("first", 0), ("first", 1), ("half",), ("first", 2), ("first", 3), ("gram",), ("line", 0),
    ("line", 1), ("sum", 0), ("line", 2), ("plane", 0, 0), ("plane", 0, 1), ("sum", 1),
    ("plane", 1, 0), ("plane", 1, 1), ("planed", 0), ("pass", 0, 0), ("sum", 2), ("line", 3),
    ("planed", 1), ("pass", 0, 1), ("pass", 0, 2), ("plane", 2, 0), ("plane", 2, 1), ("pass", 1, 0),
    ("sum", 3), ("pass", 0, 3), ("plane", 3, 0), ("plane", 3, 1), ("sum", 4), ("far", 0, 0),
    ("eliminate", 0), ("eliminate", 1), ("eliminate", 2), ("far", 0, 1), ("planed", 2),
    ("far", 0, 2), ("pass", 1, 1), ("pass", 1, 2), ("far", 0, 3), ("pass", 1, 3), ("far", 1, 0),
    ("pass", 2, 0), ("eliminate", 3), ("share", 0), ("planed", 3), ("pass", 2, 1), ("pass", 3, 0),
    ("multiply", 0, 0, 1), ("pass", 2, 2), ("pass", 2, 3), ("far", 1, 1), ("far", 1, 2),
    ("far", 1, 3), ("pass", 3, 1), ("pass", 3, 2), ("far", 2, 0), ("multiply", 0, 1, 2),
    ("pass", 3, 3), ("far", 2, 1), ("share", 1), ("multiply", 1, 0, 1), ("far", 3, 0),
    ("far", 2, 2), ("far", 2, 3), ("multiply", 1, 1, 2), ("far", 3, 1), ("far", 3, 2), ("share", 2),
    ("multiply", 2, 0, 1), ("far", 3, 3), ("multiply", 2, 1, 2), ("share", 3),
    ("multiply", 3, 0, 2),
)


def position():
    host, chip = lax.axis_index("hst"), lax.axis_index("chip")
    return (host // RING, lax.rem(host, RING), chip // 2), lax.rem(chip, 2)


class Links:
    def __init__(self, send, recv):
        self.send, self.recv = send, recv
        self.pos, self.core = position()
        self.send_ids, self.recv_ids = {}, {}

    def at(self, axis, delta):
        return lax.rem(self.pos[axis] + delta, RING)

    def device(self, axis=None, delta=0):
        place = list(self.pos)
        core = self.core
        if axis is None:
            core = 1 - core
        else:
            place[axis] = self.at(axis, delta)
        return (place[0] * RING + place[1], place[2] * 2 + core)

    def copy(self, out, into, src, dst, device):
        return pltpu.make_async_remote_copy(
            src_ref=src,
            dst_ref=dst,
            send_sem=self.send.at[self.send_ids.setdefault(out, len(self.send_ids))],
            recv_sem=self.recv.at[self.recv_ids.setdefault(into, len(self.recv_ids))],
            device_id=device,
            device_id_type=MESH,
        )

    def wait(self, into, like):
        self.copy(next(iter(self.send_ids)), into, like, like, self.device()).wait_recv()

    def wait_sent(self, out, like):
        self.copy(out, next(iter(self.recv_ids)), like, like, self.device()).wait_send()


class Gather(Links):
    def __init__(self, waves, send, recv):
        super().__init__(send, recv)
        self.waves = waves

    def view(self, w, t, axes):
        first, rows = ROWS[w][t]
        index = [axes.get(axis, self.pos[axis]) for axis in range(3)]
        return self.waves[w].at[index[0], index[1], index[2], self.core, pl.ds(first, rows), :]

    def blocks(self, w, y, x, z):
        return self.waves[w].at[pl.ds(0, y), pl.ds(0, x), pl.ds(0, z), 0]

    def push(self, out, into, w, t, axes, device):
        view = self.view(w, t, axes)
        self.copy(out, (w, into), view, view, device).start()

    def line(self, t, second=None, third=None, half=ALL):
        axes = {ORDER[t][0]: half}
        if second is not None:
            axes[ORDER[t][1]] = second
        if third is not None:
            axes[ORDER[t][2]] = third
        return axes

    def seconds(self, t):
        return [self.at(ORDER[t][1], delta) for delta in (0, 3, 1, 2)]

    def first_start(self, w):
        for t in range(3):
            for delta in (2, 1, 3):
                into = "opposite" if delta == 2 else "first"
                self.push("first", into, w, t, {}, self.device(ORDER[t][0], delta))
        if w in EARLY:
            self.block(w, {})

    def block(self, w, *blocks):
        for step in (1, 2):
            for t in range(3):
                for delta in (1, 3):
                    into = ("second", delta) if step == 1 else ("third", 0)
                    device = self.device(ORDER[t][step], delta)
                    for axes in blocks:
                        out = "second" if step == 1 else "third"
                        self.push(out, into, w, t, axes if axes == {} else axes[t], device)

    def third_line(self, w, t, j):
        axes = self.line(t, self.seconds(t)[j])
        for delta in (1, 3):
            self.push("third", ("third", j), w, t, axes, self.device(ORDER[t][2], delta))
        self.sibling(w, t, j, 0)

    def sibling(self, w, t, j, away):
        axes = self.line(t, self.seconds(t)[j], self.at(ORDER[t][2], 4 - away))
        if w in WHOLE and away != 2:
            if j < 3:
                return
            axes = self.line(t, ALL, self.at(ORDER[t][2], 4 - away))
        self.push("share", "share", w, t, axes, self.device())

    def sibling_end(self, w):
        self.wait((w, "share"), self.blocks(w, 4, 4, 4))

    def first_end(self, w):
        from_start = [
            [{ORDER[t][0]: self.at(ORDER[t][0], delta)} for t in range(3)] for delta in (3, 1, 2)
        ]
        self.wait((w, "first"), self.blocks(w, 1, 1, 2))
        if w in EARLY:
            self.block(w, *from_start[:2])
        self.wait((w, "opposite"), self.blocks(w, 1, 1, 1))
        if w in EARLY:
            self.block(w, from_start[2])
            for t in range(3):
                self.sibling(w, t, 0, 0)
            return
        for t in range(3):
            for delta in (1, 3):
                device = self.device(ORDER[t][1], delta)
                self.push("second", ("second", delta), w, t, self.line(t), device)
        for t in range(3):
            self.third_line(w, t, 0)

    def second_pass(self, w, k):
        delta, half = HALVES[k]
        self.wait((w, ("second", delta)), self.blocks(w, 1, 1, 4))
        for t in range(3):
            axes = self.line(t, self.seconds(t)[k + 1], half=half)
            self.push("second", "halves", w, t, axes, self.device(ORDER[t][1], delta))
        for t in range(3):
            self.third_line(w, t, k + 1)

    def second_end(self, w):
        self.wait((w, "halves"), self.blocks(w, 1, 1, 4))
        for t in range(3):
            self.third_line(w, t, 3)

    def third_pass(self, w, j):
        self.wait((w, ("third", j)), self.blocks(w, 1, 2, 4))
        for t in range(3):
            axis, source = ORDER[t][2], self.seconds(t)[j]
            for delta, half in HALVES:
                axes = self.line(t, source, self.at(axis, 4 - delta), half)
                self.push("third", ("far", j), w, t, axes, self.device(axis, delta))
        for t in range(3):
            for delta in (1, 3):
                self.sibling(w, t, j, delta)

    def third_end(self, w, j):
        self.wait((w, ("far", j)), self.blocks(w, 1, 1, 4))
        for t in range(3):
            self.sibling(w, t, j, 2)

    def finish(self, like):
        self.wait_sent("first", like.at[0, pl.ds(0, 3 * K)])
        self.wait_sent("second", like.at[pl.ds(0, 3)])
        self.wait_sent("third", like.at[pl.ds(0, 12)])
        self.wait_sent("share", like.at[pl.ds(0, 16)])

    def take(self, name, w, *more):
        step = {
            "first": self.first_start,
            "line": self.first_end,
            "plane": self.second_pass,
            "planed": self.second_end,
            "pass": self.third_pass,
            "far": self.third_end,
            "share": self.sibling_end,
        }[name]
        step(w, *more)


class Sum(Links):
    def __init__(self, sibling_half, stages, total, send, recv):
        super().__init__(send, recv)
        self.sibling_half, self.stages, self.total = sibling_half, stages, total
        self.half = K // 2

    def rows(self, core):
        return pl.ds(pl.multiple_of(core * self.half, self.half), self.half)

    def begin(self, matrix):
        self.matrix = matrix
        out = matrix.at[self.rows(1 - self.core)]
        self.copy("in", "in", out, self.sibling_half, self.device()).start()

    def stage_start(self, stage, value):
        parts = []
        for t in range(3):
            first, rows = GRAM_ROWS[t]
            axis = ORDER[t][stage]
            own = self.stages.at[stage, self.pos[axis], pl.ds(first, rows)]
            own[...] = value[first : first + rows]
            parts.append((axis, own))
        for delta in (2, 1, 3):
            for axis, own in parts:
                self.copy(stage, stage, own, own, self.device(axis, delta)).start()

    def stage_end(self, stage):
        self.wait(stage, self.stages.at[stage, pl.ds(0, 3)])
        slots = [self.stages[stage, p] for p in range(RING)]
        return (slots[0] + slots[1]) + (slots[2] + slots[3])

    def take(self, step):
        if step == 0:
            self.wait("in", self.sibling_half)
            self.stage_start(0, self.matrix[self.rows(self.core)] + self.sibling_half[...])
        elif step < 3:
            self.stage_start(step, self.stage_end(step - 1))
        elif step == 3:
            mine = self.total.at[self.rows(self.core)]
            mine[...] = self.stage_end(2)
            self.copy("out", "out", mine, mine, self.device()).start()
        else:
            self.wait("out", self.total.at[self.rows(1 - self.core)])

    def finish(self):
        for stage in range(3):
            self.wait_sent(stage, self.stages.at[stage, pl.ds(0, 3)])
        self.wait_sent("in", self.sibling_half)
        self.wait_sent("out", self.total.at[self.rows(self.core)])


def product(left, right, left_dim, right_dim):
    dims = (((left_dim,), (right_dim,)), ((), ()))
    return lax.dot_general(left, right, dims, precision=HIGHEST, preferred_element_type=jnp.float32)


def factor_inverse(matrix, result, panel=32, pivots=8):
    ids = [lax.broadcasted_iota(jnp.int32, (K, K), dim) for dim in (0, 1)]
    side = jnp.where(ids[0] == ids[1], 1.0, 0.0)
    row = lax.broadcasted_iota(jnp.int32, (panel, K), 0)
    lane = lax.broadcasted_iota(jnp.int32, (panel, K), 1)
    uppers, inverses = [], []
    for first in range(0, K, panel):
        a, w = matrix[:panel], side[:panel]
        for j in range(0, panel, pivots):
            span = range(pivots)
            cols = [
                jnp.broadcast_to(a[:, first + j + q : first + j + q + 1], (panel, K)) for q in span
            ]
            row_a = [a[j + q : j + q + 1] for q in span]
            row_w = [w[j + q : j + q + 1] for q in span]
            small = [[cols[k][j + q : j + q + 1] for k in span] for q in span]
            for q in span:
                inverse = 1.0 / small[q][q]
                ratio = {k: small[q][k] * inverse for k in range(q + 1, pivots)}
                for k in range(q + 1, pivots):
                    for m in range(k, pivots):
                        small[k][m] = small[k][m] - ratio[k] * small[q][m]
                    row_a[k] = row_a[k] - ratio[k] * row_a[q]
                    row_w[k] = row_w[k] - ratio[k] * row_w[q]
                weight = jnp.where(row > j + q, cols[q], 0.0) * inverse
                for k in range(q + 1, pivots):
                    cols[k] = cols[k] - cols[q] * ratio[k]
                a = a - weight * row_a[q]
                w = w - weight * row_w[q]
        diagonal = jnp.sum(jnp.where(lane == row + first, a, 0.0), axis=1, keepdims=True)
        scale = lax.rsqrt(diagonal)
        a = jnp.where(lane >= row + first, a * scale, 0.0)
        w = w * scale
        uppers.append(a)
        inverses.append(w)
        if first + panel < K:
            rest = a[:, first + panel :]
            matrix = matrix[panel:] - product(rest, a, 0, 0)
            side = side[panel:] - product(rest, w, 0, 0)
        yield
    result.extend((jnp.concatenate(uppers, axis=0), jnp.concatenate(inverses, axis=0)))


def kernel(
    cols_hbm,
    live_hbm,
    tiles_hbm,
    degree_hbm,
    basis_hbm,
    image_hbm,
    sum_hbm,
    cols,
    live,
    degree,
    basis,
    tiles,
    a0,
    a1,
    a2,
    a3,
    b0,
    b1,
    b2,
    b3,
    scale,
    total,
    gram,
    half_one,
    stages_one,
    sum_one,
    half_two,
    stages_two,
    sum_two,
    load_sem,
    send_a,
    recv_a,
    send_b,
    recv_b,
    send_g,
    recv_g,
    send_h,
    recv_h,
):
    items = float(BLK * 2 * RING**3)
    first = Gather((a0, a1, a2, a3), send_a, recv_a)
    second = Gather((b0, b1, b2, b3), send_b, recv_b)
    gram_one = Sum(half_one, stages_one, sum_one, send_g, recv_g)
    gram_two = Sum(half_two, stages_two, sum_two, send_h, recv_h)
    pos, core = first.pos, first.core

    barrier = pltpu.get_barrier_semaphore()
    near = [first.device()] + [first.device(axis, d) for axis in range(3) for d in (1, 2, 3)]
    for device in near:
        pl.semaphore_signal(barrier, inc=1, device_id=device, device_id_type=MESH)
    pairs = [(degree_hbm, degree), (basis_hbm, basis), (cols_hbm, cols), (live_hbm, live)]
    pairs += [(tiles_hbm.at[pl.ds(8 * i, 8)], tiles.at[pl.ds(8 * i, 8)]) for i in range(4)]
    loads = [pltpu.make_async_copy(*pair, load_sem.at[i]) for i, pair in enumerate(pairs)]
    for load in loads:
        load.start()

    def place(waves, w, value):
        waves[w][pos[0], pos[1], pos[2], core] = value.astype(jnp.bfloat16)

    loads[0].wait()
    for i in range(BLK // K):
        row_scale = 1.0 / jnp.sqrt(degree[pl.ds(i * K, K)].astype(jnp.float32))
        scale[pl.ds(i * K, K)] = jnp.broadcast_to(row_scale.reshape(1, K), (K, K)).T
    loads[1].wait()
    for w in range(WAVES):
        rows = pl.ds(w * DEPTH, DEPTH)
        place(first.waves, w, scale[rows] * basis[rows].astype(jnp.float32))
    pl.semaphore_wait(barrier, len(near))

    def multiply(waves, w, groups, rows=pl.ds(0, BLK)):
        @pl.loop(*groups)
        def _(group):
            parts = []
            for u in range(GROUP):
                slot = group * GROUP + u
                col = cols[slot]
                picked = waves[w][
                    col // 32, lax.rem(col // 8, 4), lax.rem(col // 2, 4), lax.rem(col, 2)
                ]
                picked = jnp.where(slot < live[0], picked, jnp.zeros_like(picked))
                tile = tiles[slot, rows, pl.ds(w * DEPTH, DEPTH)]
                parts.append(jnp.dot(tile, picked, preferred_element_type=jnp.float32))
            while len(parts) > 1:
                parts = [left + right for left, right in zip(parts[::2], parts[1::2])]
            total[rows] += parts[0]

    total[...] = jnp.zeros_like(total)
    for name, *more in ROUND_ONE:
        if name == "multiply":
            multiply(first.waves, more[0], more[1:])
        elif name == "loaded":
            for load in loads[2:]:
                load.wait()
        else:
            first.take(name, *more)

    def half_image(half):
        rows = pl.ds(half * (BLK // 2), BLK // 2)
        multiply(first.waves, WAVES - 1, (0, SLOTS // GROUP), rows)
        image = total[rows] * scale[rows]
        total[rows] = image
        image = scale[rows] * image
        for w in range(WAVES // 2):
            place(second.waves, half * (WAVES // 2) + w, image[w * DEPTH : (w + 1) * DEPTH])

    factors = []
    half_image(0)
    for name, *more in ROUND_TWO:
        if name == "half":
            half_image(1)
        elif name == "gram":
            image = total[...]
            total[...] = jnp.zeros_like(total)
            gram[...] = product(image, image, 0, 0) * (1.0 / items)
            gram_one.begin(gram)
        elif name == "sum":
            gram_one.take(more[0])
        elif name == "eliminate":
            if more[0] == 0:
                elimination = factor_inverse(sum_one[...], factors)
            next(elimination)
        elif name == "multiply":
            multiply(second.waves, more[0], more[1:])
        else:
            second.take(name, *more)
    next(elimination, None)
    raw = total[...] * scale[...]
    image = product(raw, factors[1], 1, 1)
    total[...] = image
    out = pltpu.make_async_copy(total, image_hbm, load_sem.at[0])
    out.start()
    gram_one.finish()
    gram[...] = product(image, image, 0, 0) * (1.0 / items)
    gram_two.begin(gram)
    for step in range(5):
        gram_two.take(step)
    out_sum = pltpu.make_async_copy(sum_two, sum_hbm, load_sem.at[1])
    out_sum.start()
    first.finish(tiles)
    second.finish(tiles)
    gram_two.finish()
    out.wait()
    out_sum.wait()


def finish(image, gram, leading, factor):
    factors = []
    for _ in factor_inverse(gram[...], factors, panel=64):
        pass
    upper, inverse = factors
    factor[...] = upper.T
    leading[...] = product(image[...], inverse, 1, 1)


def local(tile_data, tile_col, live_count, degree, start_basis):
    vmem, anywhere = pl.BlockSpec(memory_space=pltpu.VMEM), pl.BlockSpec(memory_space=pl.ANY)
    wave = pltpu.VMEM((RING, RING, RING, 2, DEPTH, K), jnp.bfloat16)
    sums = [
        pltpu.VMEM((K // 2, K), jnp.float32),
        pltpu.VMEM((3, RING, K // 2, K), jnp.float32),
        pltpu.VMEM((K, K), jnp.float32),
    ]
    dma = pltpu.SemaphoreType.DMA
    rows = jax.ShapeDtypeStruct((BLK, K), jnp.float32)
    square = jax.ShapeDtypeStruct((K, K), jnp.float32)
    image, gram = pl.pallas_call(
        kernel,
        out_shape=(rows, square),
        in_specs=[anywhere] * 5,
        out_specs=(anywhere, anywhere),
        scratch_shapes=[
            pltpu.SMEM((SLOTS,), jnp.int32),
            pltpu.SMEM((1,), jnp.int32),
            pltpu.VMEM((BLK,), jnp.int32),
            pltpu.VMEM((BLK, K), jnp.bfloat16),
            pltpu.VMEM((SLOTS, BLK, BLK), jnp.bfloat16),
            *[wave] * (2 * WAVES),
            pltpu.VMEM((BLK, K), jnp.float32),
            pltpu.VMEM((BLK, K), jnp.float32),
            pltpu.VMEM((K, K), jnp.float32),
            *sums * 2,
            dma((8,)),
            *[dma((SENDS,)), dma((RECEIPTS,))] * 2,
            *[dma((SUMS,))] * 4,
        ],
        compiler_params=pltpu.CompilerParams(
            collective_id=0, has_side_effects=True, vmem_limit_bytes=58 * 2**20
        ),
        name="two_rounds",
    )(tile_col, live_count, tile_data, degree, start_basis)
    return pl.pallas_call(
        finish,
        out_shape=(rows, square),
        in_specs=[vmem] * 2,
        out_specs=(vmem, vmem),
        name="finish",
    )(image, gram)


def solution(mesh):
    placed = (
        P(("hst", "chip"), None, None),
        P(("hst", "chip")),
        P(("hst", "chip")),
        P(("hst", "chip")),
        P(("hst", "chip"), None),
    )
    return jax.shard_map(
        local,
        mesh=mesh,
        in_specs=placed,
        out_specs=(P(("hst", "chip"), None), P()),
        check_vma=False,
    )
```

```python
import functools

import jax
import jax.numpy as jnp
from jax import lax
from jax.experimental import pallas as pl
from jax.experimental.pallas import tpu as pltpu
from jax.sharding import PartitionSpec as P

BLK = 512
K = 128
SLOTS = 32
RING = 4
WAVES = 4
DEPTH = BLK // WAVES
MESH = pl.DeviceIdType.MESH
HIGHEST = lax.Precision.HIGHEST
ALL = pl.ds(0, RING)
HALVES = ((1, pl.ds(0, 2)), (3, pl.ds(2, 2)))
ORDER = ((1, 0, 2), (0, 2, 1), (2, 1, 0))
ROWS = (
    ((0, 48), (48, 48), (96, 32)),
    ((0, 32), (32, 48), (80, 48)),
    ((0, 48), (48, 32), (80, 48)),
    ((0, 48), (48, 48), (96, 32)),
)
GRAM_ROWS = ((0, 24), (24, 24), (48, 16))
SENDS = 4
RECEIPTS = 56
SUMS = 3
GROUP = 16
WHOLE = (0, 1, 2)
EARLY = (0, 1)
ROUND_ONE = (
    ("first", 0), ("first", 2), ("first", 1), ("first", 3), ("line", 0), ("line", 1), ("line", 2),
    ("plane", 0, 0), ("plane", 0, 1), ("plane", 2, 0), ("line", 3), ("plane", 1, 0), ("planed", 0),
    ("plane", 1, 1), ("pass", 0, 0), ("pass", 0, 1), ("plane", 2, 1), ("planed", 1), ("pass", 0, 2),
    ("pass", 1, 0), ("pass", 0, 3), ("planed", 2), ("plane", 3, 0), ("plane", 3, 1), ("far", 0, 0),
    ("far", 0, 1), ("pass", 1, 1), ("far", 0, 2), ("far", 1, 0), ("pass", 1, 2), ("far", 0, 3),
    ("pass", 2, 0), ("pass", 1, 3), ("pass", 2, 1), ("share", 0), ("loaded",),
    ("multiply", 0, 0, 1), ("planed", 3), ("pass", 2, 2), ("pass", 2, 3), ("pass", 3, 0),
    ("far", 1, 1), ("multiply", 0, 1, 2), ("far", 1, 2), ("far", 1, 3), ("far", 2, 0),
    ("pass", 3, 1), ("pass", 3, 2), ("share", 1), ("far", 2, 1), ("pass", 3, 3),
    ("multiply", 1, 0, 1), ("far", 2, 2), ("far", 2, 3), ("multiply", 1, 1, 2), ("far", 3, 0),
    ("far", 3, 1), ("share", 2), ("multiply", 2, 0, 1), ("far", 3, 2), ("far", 3, 3),
    ("multiply", 2, 1, 2), ("share", 3),
)
ROUND_TWO = (
    ("first", 0), ("first", 1), ("half",), ("first", 2), ("first", 3), ("gram",), ("line", 0),
    ("line", 1), ("line", 2), ("sum", 0), ("plane", 0, 0), ("line", 3), ("plane", 0, 1), ("sum", 1),
    ("plane", 1, 0), ("plane", 1, 1), ("planed", 0), ("plane", 2, 0), ("pass", 0, 0), ("planed", 1),
    ("pass", 0, 1), ("plane", 2, 1), ("pass", 0, 2), ("pass", 1, 0), ("sum", 2), ("plane", 3, 0),
    ("pass", 1, 1), ("eliminate", 0), ("eliminate", 1), ("pass", 0, 3), ("eliminate", 2),
    ("plane", 3, 1), ("pass", 1, 2), ("planed", 2), ("eliminate", 3), ("far", 1, 0), ("pass", 1, 3),
    ("far", 0, 0), ("far", 0, 1), ("far", 0, 2), ("pass", 2, 0), ("far", 0, 3), ("far", 1, 1),
    ("planed", 3), ("pass", 2, 1), ("pass", 3, 0), ("share", 0), ("multiply", 0, 0, 1),
    ("far", 1, 2), ("pass", 2, 2), ("pass", 2, 3), ("far", 1, 3), ("pass", 3, 1), ("pass", 3, 2),
    ("multiply", 0, 1, 2), ("pass", 3, 3), ("far", 2, 0), ("far", 2, 1), ("share", 1),
    ("multiply", 1, 0, 1), ("far", 2, 2), ("far", 3, 0), ("far", 2, 3), ("multiply", 1, 1, 2),
    ("far", 3, 1), ("share", 2), ("far", 3, 2), ("multiply", 2, 0, 1), ("far", 3, 3),
    ("multiply", 2, 1, 2), ("share", 3), ("multiply", 3, 0, 2),
)


def position():
    host, chip = lax.axis_index("hst"), lax.axis_index("chip")
    return (host // RING, lax.rem(host, RING), chip // 2), lax.rem(chip, 2)


class Links:
    def __init__(self, send, recv):
        self.send, self.recv = send, recv
        self.pos, self.core = position()
        self.send_ids, self.recv_ids = {}, {}

    def at(self, axis, delta):
        return lax.rem(self.pos[axis] + delta, RING)

    def device(self, axis=None, delta=0, core=None):
        place = list(self.pos)
        if axis is None:
            core = 1 - self.core
        else:
            core = self.core if core is None else core
            place[axis] = self.at(axis, delta)
        return (place[0] * RING + place[1], place[2] * 2 + core)

    def copy(self, out, into, src, dst, device):
        return pltpu.make_async_remote_copy(
            src_ref=src,
            dst_ref=dst,
            send_sem=self.send.at[self.send_ids.setdefault(out, len(self.send_ids))],
            recv_sem=self.recv.at[self.recv_ids.setdefault(into, len(self.recv_ids))],
            device_id=device,
            device_id_type=MESH,
        )

    def wait(self, into, like):
        self.copy(next(iter(self.send_ids)), into, like, like, self.device()).wait_recv()

    def wait_sent(self, out, like):
        self.copy(out, next(iter(self.recv_ids)), like, like, self.device()).wait_send()


class Gather(Links):
    def __init__(self, waves, send, recv):
        super().__init__(send, recv)
        self.waves = waves

    def view(self, w, t, axes):
        first, rows = ROWS[w][t]
        index = [axes.get(axis, self.pos[axis]) for axis in range(3)]
        return self.waves[w].at[index[0], index[1], index[2], self.core, pl.ds(first, rows), :]

    def blocks(self, w, y, x, z):
        return self.waves[w].at[pl.ds(0, y), pl.ds(0, x), pl.ds(0, z), 0]

    def push(self, out, into, w, t, axes, device):
        view = self.view(w, t, axes)
        self.copy(out, (w, into), view, view, device).start()

    def line(self, t, second=None, third=None, half=ALL):
        axes = {ORDER[t][0]: half}
        if second is not None:
            axes[ORDER[t][1]] = second
        if third is not None:
            axes[ORDER[t][2]] = third
        return axes

    def seconds(self, t):
        return [self.at(ORDER[t][1], delta) for delta in (0, 3, 1, 2)]

    def first_start(self, w):
        for t in range(3):
            for delta in (2, 1, 3):
                into = "opposite" if delta == 2 else "first"
                self.push("first", into, w, t, {}, self.device(ORDER[t][0], delta))
        if w in EARLY:
            self.block(w, {})

    def block(self, w, *blocks):
        for step in (1, 2):
            for t in range(3):
                for delta in (1, 3):
                    into = ("second", delta) if step == 1 else ("third", 0)
                    device = self.device(ORDER[t][step], delta)
                    for axes in blocks:
                        out = "second" if step == 1 else "third"
                        self.push(out, into, w, t, axes if axes == {} else axes[t], device)

    def third_line(self, w, t, j):
        axes = self.line(t, self.seconds(t)[j])
        for delta in (1, 3):
            self.push("third", ("third", j), w, t, axes, self.device(ORDER[t][2], delta))
        self.sibling(w, t, j, 0)

    def sibling(self, w, t, j, away):
        axes = self.line(t, self.seconds(t)[j], self.at(ORDER[t][2], 4 - away))
        if w in WHOLE and away != 2:
            if j < 3:
                return
            axes = self.line(t, ALL, self.at(ORDER[t][2], 4 - away))
        self.push("share", "share", w, t, axes, self.device())

    def sibling_end(self, w):
        self.wait((w, "share"), self.blocks(w, 4, 4, 4))

    def first_end(self, w):
        from_start = [
            [{ORDER[t][0]: self.at(ORDER[t][0], delta)} for t in range(3)] for delta in (3, 1, 2)
        ]
        self.wait((w, "first"), self.blocks(w, 1, 1, 2))
        if w in EARLY:
            self.block(w, *from_start[:2])
        self.wait((w, "opposite"), self.blocks(w, 1, 1, 1))
        if w in EARLY:
            self.block(w, from_start[2])
            for t in range(3):
                self.sibling(w, t, 0, 0)
            return
        for t in range(3):
            for delta in (1, 3):
                device = self.device(ORDER[t][1], delta)
                self.push("second", ("second", delta), w, t, self.line(t), device)
        for t in range(3):
            self.third_line(w, t, 0)

    def second_pass(self, w, k):
        delta, half = HALVES[k]
        self.wait((w, ("second", delta)), self.blocks(w, 1, 1, 4))
        for t in range(3):
            axes = self.line(t, self.seconds(t)[k + 1], half=half)
            self.push("second", "halves", w, t, axes, self.device(ORDER[t][1], delta))
        for t in range(3):
            self.third_line(w, t, k + 1)

    def second_end(self, w):
        self.wait((w, "halves"), self.blocks(w, 1, 1, 4))
        for t in range(3):
            self.third_line(w, t, 3)

    def third_pass(self, w, j):
        self.wait((w, ("third", j)), self.blocks(w, 1, 2, 4))
        for t in range(3):
            axis, source = ORDER[t][2], self.seconds(t)[j]
            for delta, half in HALVES:
                axes = self.line(t, source, self.at(axis, 4 - delta), half)
                self.push("third", ("far", j), w, t, axes, self.device(axis, delta))
        for t in range(3):
            for delta in (1, 3):
                self.sibling(w, t, j, delta)

    def third_end(self, w, j):
        self.wait((w, ("far", j)), self.blocks(w, 1, 1, 4))
        for t in range(3):
            self.sibling(w, t, j, 2)

    def finish(self, like):
        self.wait_sent("first", like.at[0, pl.ds(0, 3 * K)])
        self.wait_sent("second", like.at[pl.ds(0, 3)])
        self.wait_sent("third", like.at[pl.ds(0, 12)])
        self.wait_sent("share", like.at[pl.ds(0, 16)])

    def take(self, name, w, *more):
        step = {
            "first": self.first_start,
            "line": self.first_end,
            "plane": self.second_pass,
            "planed": self.second_end,
            "pass": self.third_pass,
            "far": self.third_end,
            "share": self.sibling_end,
        }[name]
        step(w, *more)


class Sum(Links):
    def __init__(self, stages, send, recv):
        super().__init__(send, recv)
        self.stages = stages
        self.half = K // 2

    def spread(self, stage, parts):
        for delta in (2, 1, 3):
            for axis, copies in parts:
                for core, source, target in copies:
                    self.copy(stage, stage, source, target, self.device(axis, delta, core)).start()

    def begin(self, matrix):
        parts = []
        for t in range(3):
            first, rows = GRAM_ROWS[t]
            axis = ORDER[t][0]
            target = self.stages[0].at[self.pos[axis] * 2 + self.core, pl.ds(first, rows)]
            copies = []
            for core in (self.core, 1 - self.core):
                start = pl.multiple_of(core * self.half + first, 8)
                copies.append((core, matrix.at[pl.ds(start, rows)], target))
            target[...] = copies[0][1][...]
            self.copy(0, 0, copies[1][1], target, self.device()).start()
            parts.append((axis, copies))
        self.spread(0, parts)

    def stage_start(self, stage, value):
        parts = []
        for t in range(3):
            first, rows = GRAM_ROWS[t]
            axis = ORDER[t][stage]
            slot = self.pos[axis] if stage == 1 else self.core * RING + self.pos[axis]
            own = self.stages[stage].at[slot, pl.ds(first, rows)]
            own[...] = value[first : first + rows]
            if stage == 2:
                self.copy(2, 2, own, own, self.device()).start()
            cores = (self.core,) if stage == 1 else (self.core, 1 - self.core)
            parts.append((axis, [(core, own, own) for core in cores]))
        self.spread(stage, parts)

    def stage_end(self, stage):
        slots = self.stages[stage]
        count = slots.shape[0]
        self.wait(stage, slots.at[pl.ds(0, count - 1)])
        sums = [slots[2 * i] + slots[2 * i + 1] for i in range(count // 2)]
        return [sums[2 * i] + sums[2 * i + 1] for i in range(count // 4)]

    def take(self, step):
        parts = self.stage_end(step)
        if step == 0:
            self.stage_start(1, parts[0] + parts[1])
        elif step == 1:
            self.stage_start(2, parts[0])
        else:
            self.total = jnp.concatenate(parts, axis=0)

    def finish(self):
        for stage, slots in enumerate(self.stages):
            self.wait_sent(stage, slots.at[pl.ds(0, slots.shape[0] - 1)])


def product(left, right, left_dim, right_dim):
    dims = (((left_dim,), (right_dim,)), ((), ()))
    return lax.dot_general(left, right, dims, precision=HIGHEST, preferred_element_type=jnp.float32)


def factor_inverse(matrix, result, panel=32, pivots=8):
    ids = [lax.broadcasted_iota(jnp.int32, (K, K), dim) for dim in (0, 1)]
    side = jnp.where(ids[0] == ids[1], 1.0, 0.0)
    row = lax.broadcasted_iota(jnp.int32, (panel, K), 0)
    lane = lax.broadcasted_iota(jnp.int32, (panel, K), 1)
    uppers, inverses = [], []
    for first in range(0, K, panel):
        a, w = matrix[:panel], side[:panel]
        done_a, done_w = [], []
        for j in range(0, panel, pivots):
            span, left = range(pivots), panel - j
            at = first + j
            cols = [jnp.broadcast_to(a[:, at + q : at + q + 1], (left, K)) for q in span]
            row_a, row_w = [a[q : q + 1] for q in span], [w[q : q + 1] for q in span]
            small = [[cols[k][q : q + 1] for k in span] for q in span]
            below = left > pivots
            if below:
                cols, a, w = [col[pivots:] for col in cols], a[pivots:], w[pivots:]
            for q in span:
                inverse = 1.0 / small[q][q]
                ratio = {k: small[q][k] * inverse for k in range(q + 1, pivots)}
                for k in range(q + 1, pivots):
                    for m in range(k, pivots):
                        small[k][m] = small[k][m] - ratio[k] * small[q][m]
                    row_a[k] = row_a[k] - ratio[k] * row_a[q]
                    row_w[k] = row_w[k] - ratio[k] * row_w[q]
                if below:
                    weight = cols[q] * inverse
                    for k in range(q + 1, pivots):
                        cols[k] = cols[k] - cols[q] * ratio[k]
                    a = a - weight * row_a[q]
                    w = w - weight * row_w[q]
                root = lax.rsqrt(small[q][q])
                done_a.append(row_a[q] * root)
                done_w.append(row_w[q] * root)
        a = jnp.where(lane >= row + first, jnp.concatenate(done_a, axis=0), 0.0)
        w = jnp.concatenate(done_w, axis=0)
        uppers.append(a)
        inverses.append(w)
        if first + panel < K:
            rest = a[:, first + panel :]
            matrix = matrix[panel:] - product(rest, a, 0, 0)
            side = side[panel:] - product(rest, w, 0, 0)
        yield
    result.extend((jnp.concatenate(uppers, axis=0), jnp.concatenate(inverses, axis=0)))


def kernel(
    cols_hbm,
    live_hbm,
    tiles_hbm,
    degree_hbm,
    basis_hbm,
    image_hbm,
    sum_hbm,
    cols,
    live,
    degree,
    basis,
    tiles,
    a0,
    a1,
    a2,
    a3,
    b0,
    b1,
    b2,
    b3,
    scale,
    total,
    gram,
    summed,
    one_first,
    one_second,
    one_third,
    two_first,
    two_second,
    two_third,
    load_sem,
    send_a,
    recv_a,
    send_b,
    recv_b,
    send_g,
    recv_g,
    send_h,
    recv_h,
):
    items = float(BLK * 2 * RING**3)
    first = Gather((a0, a1, a2, a3), send_a, recv_a)
    second = Gather((b0, b1, b2, b3), send_b, recv_b)
    gram_one = Sum((one_first, one_second, one_third), send_g, recv_g)
    gram_two = Sum((two_first, two_second, two_third), send_h, recv_h)
    pos, core = first.pos, first.core

    barrier = pltpu.get_barrier_semaphore()
    near = [first.device()] + [
        first.device(axis, delta, c)
        for c in (core, 1 - core)
        for axis in range(3)
        for delta in (1, 2, 3)
    ]
    for device in near:
        pl.semaphore_signal(barrier, inc=1, device_id=device, device_id_type=MESH)
    pairs = [(degree_hbm, degree), (basis_hbm, basis), (cols_hbm, cols), (live_hbm, live)]
    pairs += [(tiles_hbm.at[pl.ds(8 * i, 8)], tiles.at[pl.ds(8 * i, 8)]) for i in range(4)]
    loads = [pltpu.make_async_copy(*pair, load_sem.at[i]) for i, pair in enumerate(pairs)]
    for load in loads:
        load.start()

    def place(waves, w, value):
        waves[w][pos[0], pos[1], pos[2], core] = value.astype(jnp.bfloat16)

    loads[0].wait()
    for i in range(BLK // K):
        row_scale = 1.0 / jnp.sqrt(degree[pl.ds(i * K, K)].astype(jnp.float32))
        scale[pl.ds(i * K, K)] = jnp.broadcast_to(row_scale.reshape(1, K), (K, K)).T
    loads[1].wait()
    for w in range(WAVES):
        rows = pl.ds(w * DEPTH, DEPTH)
        place(first.waves, w, scale[rows] * basis[rows].astype(jnp.float32))
    pl.semaphore_wait(barrier, len(near))

    def multiply(waves, w, groups, rows=pl.ds(0, BLK)):
        @pl.loop(*groups)
        def _(group):
            parts = []
            for u in range(GROUP):
                slot = group * GROUP + u
                col = cols[slot]
                picked = waves[w][
                    col // 32, lax.rem(col // 8, 4), lax.rem(col // 2, 4), lax.rem(col, 2)
                ]
                picked = jnp.where(slot < live[0], picked, jnp.zeros_like(picked))
                tile = tiles[slot, rows, pl.ds(w * DEPTH, DEPTH)]
                parts.append(jnp.dot(tile, picked, preferred_element_type=jnp.float32))
            while len(parts) > 1:
                parts = [left + right for left, right in zip(parts[::2], parts[1::2])]
            total[rows] += parts[0]

    total[...] = jnp.zeros_like(total)
    for name, *more in ROUND_ONE:
        if name == "multiply":
            multiply(first.waves, more[0], more[1:])
        elif name == "loaded":
            for load in loads[2:]:
                load.wait()
        else:
            first.take(name, *more)

    def half_image(half):
        rows = pl.ds(half * (BLK // 2), BLK // 2)
        multiply(first.waves, WAVES - 1, (0, SLOTS // GROUP), rows)
        image = total[rows] * scale[rows]
        total[rows] = image
        image = scale[rows] * image
        for w in range(WAVES // 2):
            place(second.waves, half * (WAVES // 2) + w, image[w * DEPTH : (w + 1) * DEPTH])

    factors = []
    half_image(0)
    for name, *more in ROUND_TWO:
        if name == "half":
            half_image(1)
        elif name == "gram":
            image = total[...]
            total[...] = jnp.zeros_like(total)
            gram[...] = product(image, image, 0, 0) * (1.0 / items)
            gram_one.begin(gram)
        elif name == "sum":
            gram_one.take(more[0])
        elif name == "eliminate":
            if more[0] == 0:
                elimination = factor_inverse(gram_one.total, factors)
            next(elimination)
        elif name == "multiply":
            multiply(second.waves, more[0], more[1:])
        else:
            second.take(name, *more)
    next(elimination, None)
    raw = total[...] * scale[...]
    image = product(raw, factors[1], 1, 1)
    total[...] = image
    out = pltpu.make_async_copy(total, image_hbm, load_sem.at[0])
    out.start()
    gram_one.finish()
    gram[...] = product(image, image, 0, 0) * (1.0 / items)
    gram_two.begin(gram)
    for step in range(3):
        gram_two.take(step)
    summed[...] = gram_two.total
    out_sum = pltpu.make_async_copy(summed, sum_hbm, load_sem.at[1])
    out_sum.start()
    first.finish(tiles)
    second.finish(tiles)
    gram_two.finish()
    out.wait()
    out_sum.wait()


def finish(image, gram, leading, factor):
    factors = []
    for _ in factor_inverse(gram[...], factors, panel=64):
        pass
    upper, inverse = factors
    factor[...] = upper.T
    leading[...] = product(image[...], inverse, 1, 1)


def local(tile_data, tile_col, live_count, degree, start_basis):
    vmem, anywhere = pl.BlockSpec(memory_space=pltpu.VMEM), pl.BlockSpec(memory_space=pl.ANY)
    wave = pltpu.VMEM((RING, RING, RING, 2, DEPTH, K), jnp.bfloat16)
    sums = [
        pltpu.VMEM((2 * RING, K // 2, K), jnp.float32),
        pltpu.VMEM((RING, K // 2, K), jnp.float32),
        pltpu.VMEM((2 * RING, K // 2, K), jnp.float32),
    ]
    dma = pltpu.SemaphoreType.DMA
    rows = jax.ShapeDtypeStruct((BLK, K), jnp.float32)
    square = jax.ShapeDtypeStruct((K, K), jnp.float32)
    image, gram = pl.pallas_call(
        kernel,
        out_shape=(rows, square),
        in_specs=[anywhere] * 5,
        out_specs=(anywhere, anywhere),
        scratch_shapes=[
            pltpu.SMEM((SLOTS,), jnp.int32),
            pltpu.SMEM((1,), jnp.int32),
            pltpu.VMEM((BLK,), jnp.int32),
            pltpu.VMEM((BLK, K), jnp.bfloat16),
            pltpu.VMEM((SLOTS, BLK, BLK), jnp.bfloat16),
            *[wave] * (2 * WAVES),
            pltpu.VMEM((BLK, K), jnp.float32),
            pltpu.VMEM((BLK, K), jnp.float32),
            pltpu.VMEM((K, K), jnp.float32),
            pltpu.VMEM((K, K), jnp.float32),
            *sums * 2,
            dma((8,)),
            *[dma((SENDS,)), dma((RECEIPTS,))] * 2,
            *[dma((SUMS,))] * 4,
        ],
        compiler_params=pltpu.CompilerParams(
            collective_id=0, has_side_effects=True, vmem_limit_bytes=58 * 2**20
        ),
        name="two_rounds",
    )(tile_col, live_count, tile_data, degree, start_basis)
    return pl.pallas_call(
        finish,
        out_shape=(rows, square),
        in_specs=[vmem] * 2,
        out_specs=(vmem, vmem),
        name="finish",
    )(image, gram)


def solution(mesh):
    placed = (
        P(("hst", "chip"), None, None),
        P(("hst", "chip")),
        P(("hst", "chip")),
        P(("hst", "chip")),
        P(("hst", "chip"), None),
    )
    return jax.shard_map(
        local,
        mesh=mesh,
        in_specs=placed,
        out_specs=(P(("hst", "chip"), None), P()),
        check_vma=False,
    )
```

```python
import functools

import jax
import jax.numpy as jnp
from jax import lax
from jax.experimental import pallas as pl
from jax.experimental.pallas import tpu as pltpu
from jax.sharding import PartitionSpec as P

BLK = 512
K = 128
SLOTS = 32
RING = 4
WAVES = 4
DEPTH = BLK // WAVES
MESH = pl.DeviceIdType.MESH
HIGHEST = lax.Precision.HIGHEST
ALL = pl.ds(0, RING)
HALVES = ((1, pl.ds(0, 2)), (3, pl.ds(2, 2)))
ORDER = ((1, 0, 2), (0, 2, 1), (2, 1, 0))
ROWS = (
    ((0, 48), (48, 48), (96, 32)),
    ((0, 32), (32, 48), (80, 48)),
    ((0, 48), (48, 32), (80, 48)),
    ((0, 48), (48, 48), (96, 32)),
)
GRAM_ROWS = ((0, 24), (24, 24), (48, 16))
SENDS = 4
RECEIPTS = 56
SUMS = 3
GROUP = 16
WHOLE = (0, 1)
EARLY = (0, 1, 2)
ROUND_ONE = (
    ("first", 2), ("first", 0), ("first", 1), ("first", 3), ("line", 2), ("line", 0), ("line", 1),
    ("line", 3), ("plane", 0, 0), ("plane", 2, 0), ("plane", 0, 1), ("plane", 1, 0),
    ("plane", 2, 1), ("plane", 1, 1), ("planed", 0), ("pass", 0, 0), ("plane", 3, 0),
    ("pass", 0, 1), ("planed", 1), ("plane", 3, 1), ("planed", 2), ("pass", 0, 2), ("far", 0, 0),
    ("pass", 0, 3), ("pass", 1, 0), ("pass", 1, 1), ("pass", 1, 2), ("pass", 2, 0), ("far", 0, 1),
    ("pass", 1, 3), ("planed", 3), ("pass", 2, 1), ("pass", 2, 2), ("pass", 2, 3), ("pass", 3, 0),
    ("far", 0, 2), ("far", 0, 3), ("pass", 3, 1), ("far", 1, 0), ("far", 1, 1), ("pass", 3, 2),
    ("far", 1, 2), ("share", 0), ("loaded",), ("multiply", 0, 0, 1), ("far", 1, 3),
    ("multiply", 0, 1, 2), ("pass", 3, 3), ("far", 2, 0), ("share", 1), ("far", 2, 1),
    ("multiply", 1, 0, 1), ("far", 2, 2), ("far", 2, 3), ("multiply", 1, 1, 2), ("far", 3, 0),
    ("share", 2), ("far", 3, 1), ("multiply", 2, 0, 1), ("far", 3, 2), ("far", 3, 3),
    ("multiply", 2, 1, 2), ("share", 3),
)
ROUND_TWO = (
    ("first", 0), ("first", 1), ("half",), ("first", 3), ("first", 2), ("gram",), ("line", 0),
    ("line", 1), ("line", 3), ("plane", 0, 0), ("plane", 0, 1), ("sum", 0), ("plane", 1, 0),
    ("plane", 1, 1), ("line", 2), ("sum", 1), ("planed", 0), ("pass", 0, 0), ("planed", 1),
    ("pass", 0, 1), ("plane", 2, 0), ("pass", 0, 2), ("pass", 1, 0), ("sum", 2), ("eliminate", 0),
    ("plane", 2, 1), ("eliminate", 1), ("pass", 1, 1), ("pass", 0, 3), ("far", 0, 0), ("far", 0, 1),
    ("plane", 3, 0), ("plane", 3, 1), ("eliminate", 2), ("planed", 2), ("eliminate", 3),
    ("far", 0, 2), ("pass", 2, 0), ("far", 0, 3), ("far", 1, 0), ("pass", 1, 2), ("pass", 1, 3),
    ("share", 0), ("far", 1, 1), ("planed", 3), ("pass", 2, 1), ("multiply", 0, 0, 1),
    ("pass", 2, 2), ("pass", 2, 3), ("pass", 3, 0), ("pass", 3, 1), ("far", 2, 0), ("far", 1, 2),
    ("far", 1, 3), ("pass", 3, 2), ("multiply", 0, 1, 2), ("pass", 3, 3), ("far", 2, 1),
    ("share", 1), ("multiply", 1, 0, 1), ("far", 2, 2), ("far", 2, 3), ("multiply", 1, 1, 2),
    ("far", 3, 0), ("far", 3, 1), ("share", 2), ("multiply", 2, 0, 1), ("far", 3, 2), ("far", 3, 3),
    ("multiply", 2, 1, 2), ("share", 3), ("multiply", 3, 0, 2),
)


def position():
    host, chip = lax.axis_index("hst"), lax.axis_index("chip")
    return (host // RING, lax.rem(host, RING), chip // 2), lax.rem(chip, 2)


class Links:
    def __init__(self, send, recv):
        self.send, self.recv = send, recv
        self.pos, self.core = position()
        self.send_ids, self.recv_ids = {}, {}

    def at(self, axis, delta):
        return lax.rem(self.pos[axis] + delta, RING)

    def device(self, axis=None, delta=0, core=None):
        place = list(self.pos)
        if axis is None:
            core = 1 - self.core
        else:
            core = self.core if core is None else core
            place[axis] = self.at(axis, delta)
        return (place[0] * RING + place[1], place[2] * 2 + core)

    def copy(self, out, into, src, dst, device):
        return pltpu.make_async_remote_copy(
            src_ref=src,
            dst_ref=dst,
            send_sem=self.send.at[self.send_ids.setdefault(out, len(self.send_ids))],
            recv_sem=self.recv.at[self.recv_ids.setdefault(into, len(self.recv_ids))],
            device_id=device,
            device_id_type=MESH,
        )

    def wait(self, into, like):
        self.copy(next(iter(self.send_ids)), into, like, like, self.device()).wait_recv()

    def wait_sent(self, out, like):
        self.copy(out, next(iter(self.recv_ids)), like, like, self.device()).wait_send()


class Gather(Links):
    def __init__(self, waves, send, recv):
        super().__init__(send, recv)
        self.waves = waves

    def view(self, w, t, axes):
        first, rows = ROWS[w][t]
        index = [axes.get(axis, self.pos[axis]) for axis in range(3)]
        return self.waves[w].at[index[0], index[1], index[2], self.core, pl.ds(first, rows), :]

    def blocks(self, w, y, x, z):
        return self.waves[w].at[pl.ds(0, y), pl.ds(0, x), pl.ds(0, z), 0]

    def push(self, out, into, w, t, axes, device):
        view = self.view(w, t, axes)
        self.copy(out, (w, into), view, view, device).start()

    def line(self, t, second=None, third=None, half=ALL):
        axes = {ORDER[t][0]: half}
        if second is not None:
            axes[ORDER[t][1]] = second
        if third is not None:
            axes[ORDER[t][2]] = third
        return axes

    def seconds(self, t):
        return [self.at(ORDER[t][1], delta) for delta in (0, 3, 1, 2)]

    def first_start(self, w):
        for t in range(3):
            for delta in (2, 1, 3):
                into = "opposite" if delta == 2 else "first"
                self.push("first", into, w, t, {}, self.device(ORDER[t][0], delta))
        if w in EARLY:
            self.block(w, {})

    def block(self, w, *blocks):
        for step in (1, 2):
            for t in range(3):
                for delta in (1, 3):
                    into = ("second", delta) if step == 1 else ("third", 0)
                    device = self.device(ORDER[t][step], delta)
                    for axes in blocks:
                        out = "second" if step == 1 else "third"
                        self.push(out, into, w, t, axes if axes == {} else axes[t], device)

    def third_line(self, w, t, j):
        axes = self.line(t, self.seconds(t)[j])
        for delta in (1, 3):
            self.push("third", ("third", j), w, t, axes, self.device(ORDER[t][2], delta))
        self.sibling(w, t, j, 0)

    def sibling(self, w, t, j, away):
        axes = self.line(t, self.seconds(t)[j], self.at(ORDER[t][2], 4 - away))
        if w in WHOLE and away != 2:
            if j < 3:
                return
            axes = self.line(t, ALL, self.at(ORDER[t][2], 4 - away))
        self.push("share", "share", w, t, axes, self.device())

    def sibling_end(self, w):
        self.wait((w, "share"), self.blocks(w, 4, 4, 4))

    def first_end(self, w):
        from_start = [
            [{ORDER[t][0]: self.at(ORDER[t][0], delta)} for t in range(3)] for delta in (3, 1, 2)
        ]
        self.wait((w, "first"), self.blocks(w, 1, 1, 2))
        if w in EARLY:
            self.block(w, *from_start[:2])
        self.wait((w, "opposite"), self.blocks(w, 1, 1, 1))
        if w in EARLY:
            self.block(w, from_start[2])
            for t in range(3):
                self.sibling(w, t, 0, 0)
            return
        for t in range(3):
            for delta in (1, 3):
                device = self.device(ORDER[t][1], delta)
                self.push("second", ("second", delta), w, t, self.line(t), device)
        for t in range(3):
            self.third_line(w, t, 0)

    def second_pass(self, w, k):
        delta, half = HALVES[k]
        self.wait((w, ("second", delta)), self.blocks(w, 1, 1, 4))
        for t in range(3):
            axes = self.line(t, self.seconds(t)[k + 1], half=half)
            self.push("second", "halves", w, t, axes, self.device(ORDER[t][1], delta))
        for t in range(3):
            self.third_line(w, t, k + 1)

    def second_end(self, w):
        self.wait((w, "halves"), self.blocks(w, 1, 1, 4))
        for t in range(3):
            self.third_line(w, t, 3)

    def third_pass(self, w, j):
        self.wait((w, ("third", j)), self.blocks(w, 1, 2, 4))
        for t in range(3):
            axis, source = ORDER[t][2], self.seconds(t)[j]
            for delta, half in HALVES:
                axes = self.line(t, source, self.at(axis, 4 - delta), half)
                self.push("third", ("far", j), w, t, axes, self.device(axis, delta))
        for t in range(3):
            for delta in (1, 3):
                self.sibling(w, t, j, delta)

    def third_end(self, w, j):
        self.wait((w, ("far", j)), self.blocks(w, 1, 1, 4))
        for t in range(3):
            self.sibling(w, t, j, 2)

    def finish(self, like):
        self.wait_sent("first", like.at[0, pl.ds(0, 3 * K)])
        self.wait_sent("second", like.at[pl.ds(0, 3)])
        self.wait_sent("third", like.at[pl.ds(0, 12)])
        self.wait_sent("share", like.at[pl.ds(0, 16)])

    def take(self, name, w, *more):
        step = {
            "first": self.first_start,
            "line": self.first_end,
            "plane": self.second_pass,
            "planed": self.second_end,
            "pass": self.third_pass,
            "far": self.third_end,
            "share": self.sibling_end,
        }[name]
        step(w, *more)


class Sum(Links):
    def __init__(self, stages, send, recv):
        super().__init__(send, recv)
        self.stages = stages
        self.half = K // 2

    def spread(self, stage, parts):
        for delta in (2, 1, 3):
            for axis, copies in parts:
                for core, source, target in copies:
                    self.copy(stage, stage, source, target, self.device(axis, delta, core)).start()

    def begin(self, matrix):
        parts = []
        for t in range(3):
            first, rows = GRAM_ROWS[t]
            axis = ORDER[t][0]
            target = self.stages[0].at[self.pos[axis] * 2 + self.core, pl.ds(first, rows)]
            copies = []
            for core in (self.core, 1 - self.core):
                start = pl.multiple_of(core * self.half + first, 8)
                copies.append((core, matrix.at[pl.ds(start, rows)], target))
            target[...] = copies[0][1][...]
            self.copy(0, 0, copies[1][1], target, self.device()).start()
            parts.append((axis, copies))
        self.spread(0, parts)

    def stage_start(self, stage, value):
        parts = []
        for t in range(3):
            first, rows = GRAM_ROWS[t]
            axis = ORDER[t][stage]
            slot = self.pos[axis] if stage == 1 else self.core * RING + self.pos[axis]
            own = self.stages[stage].at[slot, pl.ds(first, rows)]
            own[...] = value[first : first + rows]
            if stage == 2:
                self.copy(2, 2, own, own, self.device()).start()
            cores = (self.core,) if stage == 1 else (self.core, 1 - self.core)
            parts.append((axis, [(core, own, own) for core in cores]))
        self.spread(stage, parts)

    def stage_end(self, stage):
        slots = self.stages[stage]
        count = slots.shape[0]
        self.wait(stage, slots.at[pl.ds(0, count - 1)])
        sums = [slots[2 * i] + slots[2 * i + 1] for i in range(count // 2)]
        return [sums[2 * i] + sums[2 * i + 1] for i in range(count // 4)]

    def take(self, step):
        parts = self.stage_end(step)
        if step == 0:
            self.stage_start(1, parts[0] + parts[1])
        elif step == 1:
            self.stage_start(2, parts[0])
        else:
            self.total = jnp.concatenate(parts, axis=0)

    def finish(self):
        for stage, slots in enumerate(self.stages):
            self.wait_sent(stage, slots.at[pl.ds(0, slots.shape[0] - 1)])


def product(left, right, left_dim, right_dim):
    dims = (((left_dim,), (right_dim,)), ((), ()))
    return lax.dot_general(left, right, dims, precision=HIGHEST, preferred_element_type=jnp.float32)


def factor_inverse(matrix, result, panel=32, pivots=8):
    ids = [lax.broadcasted_iota(jnp.int32, (K, K), dim) for dim in (0, 1)]
    side = jnp.where(ids[0] == ids[1], 1.0, 0.0)
    row = lax.broadcasted_iota(jnp.int32, (panel, K), 0)
    lane = lax.broadcasted_iota(jnp.int32, (panel, K), 1)
    uppers, inverses = [], []
    for first in range(0, K, panel):
        a, w = matrix[:panel], side[:panel]
        done_a, done_w = [], []
        for j in range(0, panel, pivots):
            span, left = range(pivots), panel - j
            at = first + j
            cols = [jnp.broadcast_to(a[:, at + q : at + q + 1], (left, K)) for q in span]
            row_a, row_w = [a[q : q + 1] for q in span], [w[q : q + 1] for q in span]
            small = [[cols[k][q : q + 1] for k in span] for q in span]
            below = left > pivots
            if below:
                cols, a, w = [col[pivots:] for col in cols], a[pivots:], w[pivots:]
            for q in span:
                inverse = 1.0 / small[q][q]
                ratio = {k: small[q][k] * inverse for k in range(q + 1, pivots)}
                for k in range(q + 1, pivots):
                    for m in range(k, pivots):
                        small[k][m] = small[k][m] - ratio[k] * small[q][m]
                    row_a[k] = row_a[k] - ratio[k] * row_a[q]
                    row_w[k] = row_w[k] - ratio[k] * row_w[q]
                if below:
                    weight = cols[q] * inverse
                    for k in range(q + 1, pivots):
                        cols[k] = cols[k] - cols[q] * ratio[k]
                    a = a - weight * row_a[q]
                    w = w - weight * row_w[q]
                root = lax.rsqrt(small[q][q])
                done_a.append(row_a[q] * root)
                done_w.append(row_w[q] * root)
        a = jnp.where(lane >= row + first, jnp.concatenate(done_a, axis=0), 0.0)
        w = jnp.concatenate(done_w, axis=0)
        uppers.append(a)
        inverses.append(w)
        if first + panel < K:
            rest = a[:, first + panel :]
            matrix = matrix[panel:] - product(rest, a, 0, 0)
            side = side[panel:] - product(rest, w, 0, 0)
        yield
    result.extend((jnp.concatenate(uppers, axis=0), jnp.concatenate(inverses, axis=0)))


def kernel(
    cols_hbm,
    live_hbm,
    tiles_hbm,
    degree_hbm,
    basis_hbm,
    image_hbm,
    sum_hbm,
    cols,
    live,
    degree,
    basis,
    tiles,
    a0,
    a1,
    a2,
    a3,
    b0,
    b1,
    b2,
    b3,
    scale,
    total,
    gram,
    summed,
    one_first,
    one_second,
    one_third,
    two_first,
    two_second,
    two_third,
    load_sem,
    send_a,
    recv_a,
    send_b,
    recv_b,
    send_g,
    recv_g,
    send_h,
    recv_h,
):
    items = float(BLK * 2 * RING**3)
    first = Gather((a0, a1, a2, a3), send_a, recv_a)
    second = Gather((b0, b1, b2, b3), send_b, recv_b)
    gram_one = Sum((one_first, one_second, one_third), send_g, recv_g)
    gram_two = Sum((two_first, two_second, two_third), send_h, recv_h)
    pos, core = first.pos, first.core

    barrier = pltpu.get_barrier_semaphore()
    near = [first.device()] + [
        first.device(axis, delta, c)
        for c in (core, 1 - core)
        for axis in range(3)
        for delta in (1, 2, 3)
    ]
    for device in near:
        pl.semaphore_signal(barrier, inc=1, device_id=device, device_id_type=MESH)
    pairs = [(degree_hbm, degree), (basis_hbm, basis), (cols_hbm, cols), (live_hbm, live)]
    pairs += [(tiles_hbm.at[pl.ds(8 * i, 8)], tiles.at[pl.ds(8 * i, 8)]) for i in range(4)]
    loads = [pltpu.make_async_copy(*pair, load_sem.at[i]) for i, pair in enumerate(pairs)]
    for load in loads:
        load.start()

    def place(waves, w, value):
        waves[w][pos[0], pos[1], pos[2], core] = value.astype(jnp.bfloat16)

    loads[0].wait()
    for i in range(BLK // K):
        row_scale = 1.0 / jnp.sqrt(degree[pl.ds(i * K, K)].astype(jnp.float32))
        scale[pl.ds(i * K, K)] = jnp.broadcast_to(row_scale.reshape(1, K), (K, K)).T
    loads[1].wait()
    for w in range(WAVES):
        rows = pl.ds(w * DEPTH, DEPTH)
        place(first.waves, w, scale[rows] * basis[rows].astype(jnp.float32))
    pl.semaphore_wait(barrier, len(near))

    def multiply(waves, w, groups, rows=pl.ds(0, BLK)):
        @pl.loop(*groups)
        def _(group):
            parts = []
            for u in range(GROUP):
                slot = group * GROUP + u
                col = cols[slot]
                picked = waves[w][
                    col // 32, lax.rem(col // 8, 4), lax.rem(col // 2, 4), lax.rem(col, 2)
                ]
                picked = jnp.where(slot < live[0], picked, jnp.zeros_like(picked))
                tile = tiles[slot, rows, pl.ds(w * DEPTH, DEPTH)]
                parts.append(jnp.dot(tile, picked, preferred_element_type=jnp.float32))
            while len(parts) > 1:
                parts = [left + right for left, right in zip(parts[::2], parts[1::2])]
            total[rows] += parts[0]

    total[...] = jnp.zeros_like(total)
    for name, *more in ROUND_ONE:
        if name == "multiply":
            multiply(first.waves, more[0], more[1:])
        elif name == "loaded":
            for load in loads[2:]:
                load.wait()
        else:
            first.take(name, *more)

    def half_image(half):
        rows = pl.ds(half * (BLK // 2), BLK // 2)
        multiply(first.waves, WAVES - 1, (0, SLOTS // GROUP), rows)
        image = total[rows] * scale[rows]
        total[rows] = image
        image = scale[rows] * image
        for w in range(WAVES // 2):
            place(second.waves, half * (WAVES // 2) + w, image[w * DEPTH : (w + 1) * DEPTH])

    factors = []
    half_image(0)
    for name, *more in ROUND_TWO:
        if name == "half":
            half_image(1)
        elif name == "gram":
            image = total[...]
            total[...] = jnp.zeros_like(total)
            gram[...] = product(image, image, 0, 0) * (1.0 / items)
            gram_one.begin(gram)
        elif name == "sum":
            gram_one.take(more[0])
        elif name == "eliminate":
            if more[0] == 0:
                elimination = factor_inverse(gram_one.total, factors)
            next(elimination)
        elif name == "multiply":
            multiply(second.waves, more[0], more[1:])
        else:
            second.take(name, *more)
    next(elimination, None)
    raw = total[...] * scale[...]
    image = product(raw, factors[1], 1, 1)
    total[...] = image
    out = pltpu.make_async_copy(total, image_hbm, load_sem.at[0])
    out.start()
    gram_one.finish()
    gram[...] = product(image, image, 0, 0) * (1.0 / items)
    gram_two.begin(gram)
    for step in range(3):
        gram_two.take(step)
    summed[...] = gram_two.total
    out_sum = pltpu.make_async_copy(summed, sum_hbm, load_sem.at[1])
    out_sum.start()
    first.finish(tiles)
    second.finish(tiles)
    gram_two.finish()
    out.wait()
    out_sum.wait()


def finish(image, gram, leading, factor):
    factors = []
    for _ in factor_inverse(gram[...], factors, panel=64):
        pass
    upper, inverse = factors
    factor[...] = upper.T
    leading[...] = product(image[...], inverse, 1, 1)


def local(tile_data, tile_col, live_count, degree, start_basis):
    vmem, anywhere = pl.BlockSpec(memory_space=pltpu.VMEM), pl.BlockSpec(memory_space=pl.ANY)
    wave = pltpu.VMEM((RING, RING, RING, 2, DEPTH, K), jnp.bfloat16)
    sums = [
        pltpu.VMEM((2 * RING, K // 2, K), jnp.float32),
        pltpu.VMEM((RING, K // 2, K), jnp.float32),
        pltpu.VMEM((2 * RING, K // 2, K), jnp.float32),
    ]
    dma = pltpu.SemaphoreType.DMA
    rows = jax.ShapeDtypeStruct((BLK, K), jnp.float32)
    square = jax.ShapeDtypeStruct((K, K), jnp.float32)
    image, gram = pl.pallas_call(
        kernel,
        out_shape=(rows, square),
        in_specs=[anywhere] * 5,
        out_specs=(anywhere, anywhere),
        scratch_shapes=[
            pltpu.SMEM((SLOTS,), jnp.int32),
            pltpu.SMEM((1,), jnp.int32),
            pltpu.VMEM((BLK,), jnp.int32),
            pltpu.VMEM((BLK, K), jnp.bfloat16),
            pltpu.VMEM((SLOTS, BLK, BLK), jnp.bfloat16),
            *[wave] * (2 * WAVES),
            pltpu.VMEM((BLK, K), jnp.float32),
            pltpu.VMEM((BLK, K), jnp.float32),
            pltpu.VMEM((K, K), jnp.float32),
            pltpu.VMEM((K, K), jnp.float32),
            *sums * 2,
            dma((8,)),
            *[dma((SENDS,)), dma((RECEIPTS,))] * 2,
            *[dma((SUMS,))] * 4,
        ],
        compiler_params=pltpu.CompilerParams(
            collective_id=0, has_side_effects=True, vmem_limit_bytes=58 * 2**20
        ),
        name="two_rounds",
    )(tile_col, live_count, tile_data, degree, start_basis)
    return pl.pallas_call(
        finish,
        out_shape=(rows, square),
        in_specs=[vmem] * 2,
        out_specs=(vmem, vmem),
        name="finish",
    )(image, gram)


def solution(mesh):
    placed = (
        P(("hst", "chip"), None, None),
        P(("hst", "chip")),
        P(("hst", "chip")),
        P(("hst", "chip")),
        P(("hst", "chip"), None),
    )
    return jax.shard_map(
        local,
        mesh=mesh,
        in_specs=placed,
        out_specs=(P(("hst", "chip"), None), P()),
        check_vma=False,
    )
```

```python
import functools

import jax
import jax.numpy as jnp
from jax import lax
from jax.experimental import pallas as pl
from jax.experimental.pallas import tpu as pltpu
from jax.sharding import PartitionSpec as P

BLK = 512
K = 128
SLOTS = 32
RING = 4
WAVES = 4
DEPTH = BLK // WAVES
MESH = pl.DeviceIdType.MESH
HIGHEST = lax.Precision.HIGHEST
ALL = pl.ds(0, RING)
HALVES = ((1, pl.ds(0, 2)), (3, pl.ds(2, 2)))
ORDER = ((1, 0, 2), (0, 2, 1), (2, 1, 0))
ROWS = (
    ((0, 48), (48, 48), (96, 32)),
    ((0, 32), (32, 48), (80, 48)),
    ((0, 48), (48, 32), (80, 48)),
    ((0, 48), (48, 48), (96, 32)),
)
GRAM_ROWS = ((0, 24), (24, 24), (48, 16))
SENDS = 4
RECEIPTS = 56
SUMS = 3
GROUP = 16
WHOLE = (0, 1)
EARLY = (0, 1, 2)
ROUND_ONE = (
    ("first", 2), ("first", 0), ("first", 1), ("first", 3), ("line", 2), ("line", 0), ("line", 1),
    ("line", 3), ("plane", 0, 0), ("plane", 2, 0), ("plane", 0, 1), ("plane", 1, 0),
    ("plane", 2, 1), ("plane", 1, 1), ("planed", 0), ("pass", 0, 0), ("plane", 3, 0),
    ("pass", 0, 1), ("planed", 1), ("plane", 3, 1), ("planed", 2), ("pass", 0, 2), ("far", 0, 0),
    ("pass", 0, 3), ("pass", 1, 0), ("pass", 1, 1), ("pass", 1, 2), ("pass", 2, 0), ("far", 0, 1),
    ("pass", 1, 3), ("planed", 3), ("pass", 2, 1), ("pass", 2, 2), ("pass", 2, 3), ("pass", 3, 0),
    ("far", 0, 2), ("far", 0, 3), ("pass", 3, 1), ("far", 1, 0), ("far", 1, 1), ("pass", 3, 2),
    ("far", 1, 2), ("share", 0), ("loaded",), ("multiply", 0, 0, 1), ("far", 1, 3),
    ("multiply", 0, 1, 2), ("pass", 3, 3), ("far", 2, 0), ("share", 1), ("far", 2, 1),
    ("multiply", 1, 0, 1), ("far", 2, 2), ("far", 2, 3), ("multiply", 1, 1, 2), ("far", 3, 0),
    ("share", 2), ("far", 3, 1), ("multiply", 2, 0, 1), ("far", 3, 2), ("far", 3, 3),
    ("multiply", 2, 1, 2), ("share", 3),
)
ROUND_TWO = (
    ("first", 0), ("first", 1), ("half",), ("first", 3), ("first", 2), ("gram",), ("line", 0),
    ("line", 1), ("line", 3), ("plane", 0, 0), ("plane", 0, 1), ("sum", 0), ("plane", 1, 0),
    ("plane", 1, 1), ("line", 2), ("sum", 1), ("planed", 0), ("pass", 0, 0), ("planed", 1),
    ("pass", 0, 1), ("plane", 2, 0), ("pass", 0, 2), ("pass", 1, 0), ("sum", 2), ("eliminate", 0),
    ("plane", 2, 1), ("eliminate", 1), ("pass", 1, 1), ("pass", 0, 3), ("far", 0, 0), ("far", 0, 1),
    ("plane", 3, 0), ("plane", 3, 1), ("eliminate", 2), ("planed", 2), ("eliminate", 3),
    ("far", 0, 2), ("pass", 2, 0), ("far", 0, 3), ("far", 1, 0), ("pass", 1, 2), ("pass", 1, 3),
    ("share", 0), ("far", 1, 1), ("planed", 3), ("pass", 2, 1), ("multiply", 0, 0, 1),
    ("pass", 2, 2), ("pass", 2, 3), ("pass", 3, 0), ("pass", 3, 1), ("far", 2, 0), ("far", 1, 2),
    ("far", 1, 3), ("pass", 3, 2), ("multiply", 0, 1, 2), ("pass", 3, 3), ("far", 2, 1),
    ("share", 1), ("multiply", 1, 0, 1), ("far", 2, 2), ("far", 2, 3), ("multiply", 1, 1, 2),
    ("far", 3, 0), ("far", 3, 1), ("share", 2), ("multiply", 2, 0, 1), ("far", 3, 2), ("far", 3, 3),
    ("multiply", 2, 1, 2), ("share", 3), ("multiply", 3, 0, 2),
)


def position():
    host, chip = lax.axis_index("hst"), lax.axis_index("chip")
    return (host // RING, lax.rem(host, RING), chip // 2), lax.rem(chip, 2)


class Links:
    def __init__(self, send, recv):
        self.send, self.recv = send, recv
        self.pos, self.core = position()
        self.send_ids, self.recv_ids = {}, {}

    def at(self, axis, delta):
        return lax.rem(self.pos[axis] + delta, RING)

    def device(self, axis=None, delta=0, core=None):
        place = list(self.pos)
        if axis is None:
            core = 1 - self.core
        else:
            core = self.core if core is None else core
            place[axis] = self.at(axis, delta)
        return (place[0] * RING + place[1], place[2] * 2 + core)

    def copy(self, out, into, src, dst, device):
        return pltpu.make_async_remote_copy(
            src_ref=src,
            dst_ref=dst,
            send_sem=self.send.at[self.send_ids.setdefault(out, len(self.send_ids))],
            recv_sem=self.recv.at[self.recv_ids.setdefault(into, len(self.recv_ids))],
            device_id=device,
            device_id_type=MESH,
        )

    def wait(self, into, like):
        self.copy(next(iter(self.send_ids)), into, like, like, self.device()).wait_recv()

    def wait_sent(self, out, like):
        self.copy(out, next(iter(self.recv_ids)), like, like, self.device()).wait_send()


class Gather(Links):
    def __init__(self, waves, send, recv):
        super().__init__(send, recv)
        self.waves = waves

    def view(self, w, t, axes):
        first, rows = ROWS[w][t]
        index = [axes.get(axis, self.pos[axis]) for axis in range(3)]
        return self.waves[w].at[index[0], index[1], index[2], self.core, pl.ds(first, rows), :]

    def blocks(self, w, y, x, z):
        return self.waves[w].at[pl.ds(0, y), pl.ds(0, x), pl.ds(0, z), 0]

    def push(self, out, into, w, t, axes, device):
        view = self.view(w, t, axes)
        self.copy(out, (w, into), view, view, device).start()

    def line(self, t, second=None, third=None, half=ALL):
        axes = {ORDER[t][0]: half}
        if second is not None:
            axes[ORDER[t][1]] = second
        if third is not None:
            axes[ORDER[t][2]] = third
        return axes

    def seconds(self, t):
        return [self.at(ORDER[t][1], delta) for delta in (0, 3, 1, 2)]

    def first_start(self, w):
        for t in range(3):
            for delta in (2, 1, 3):
                into = "opposite" if delta == 2 else "first"
                self.push("first", into, w, t, {}, self.device(ORDER[t][0], delta))
        if w in EARLY:
            self.block(w, {})

    def block(self, w, *blocks):
        for step in (1, 2):
            for t in range(3):
                for delta in (1, 3):
                    into = ("second", delta) if step == 1 else ("third", 0)
                    device = self.device(ORDER[t][step], delta)
                    for axes in blocks:
                        out = "second" if step == 1 else "third"
                        self.push(out, into, w, t, axes if axes == {} else axes[t], device)

    def third_line(self, w, t, j):
        axes = self.line(t, self.seconds(t)[j])
        for delta in (1, 3):
            self.push("third", ("third", j), w, t, axes, self.device(ORDER[t][2], delta))
        self.sibling(w, t, j, 0)

    def sibling(self, w, t, j, away):
        axes = self.line(t, self.seconds(t)[j], self.at(ORDER[t][2], 4 - away))
        if w in WHOLE and away != 2:
            if j < 3:
                return
            axes = self.line(t, ALL, self.at(ORDER[t][2], 4 - away))
        self.push("share", "share", w, t, axes, self.device())

    def sibling_end(self, w):
        self.wait((w, "share"), self.blocks(w, 4, 4, 4))

    def first_end(self, w):
        from_start = [
            [{ORDER[t][0]: self.at(ORDER[t][0], delta)} for t in range(3)] for delta in (3, 1, 2)
        ]
        self.wait((w, "first"), self.blocks(w, 1, 1, 2))
        if w in EARLY:
            self.block(w, *from_start[:2])
        self.wait((w, "opposite"), self.blocks(w, 1, 1, 1))
        if w in EARLY:
            self.block(w, from_start[2])
            for t in range(3):
                self.sibling(w, t, 0, 0)
            return
        for t in range(3):
            for delta in (1, 3):
                device = self.device(ORDER[t][1], delta)
                self.push("second", ("second", delta), w, t, self.line(t), device)
        for t in range(3):
            self.third_line(w, t, 0)

    def second_pass(self, w, k):
        delta, half = HALVES[k]
        self.wait((w, ("second", delta)), self.blocks(w, 1, 1, 4))
        for t in range(3):
            axes = self.line(t, self.seconds(t)[k + 1], half=half)
            self.push("second", "halves", w, t, axes, self.device(ORDER[t][1], delta))
        for t in range(3):
            self.third_line(w, t, k + 1)

    def second_end(self, w):
        self.wait((w, "halves"), self.blocks(w, 1, 1, 4))
        for t in range(3):
            self.third_line(w, t, 3)

    def third_pass(self, w, j):
        self.wait((w, ("third", j)), self.blocks(w, 1, 2, 4))
        for t in range(3):
            axis, source = ORDER[t][2], self.seconds(t)[j]
            for delta, half in HALVES:
                axes = self.line(t, source, self.at(axis, 4 - delta), half)
                self.push("third", ("far", j), w, t, axes, self.device(axis, delta))
        for t in range(3):
            for delta in (1, 3):
                self.sibling(w, t, j, delta)

    def third_end(self, w, j):
        self.wait((w, ("far", j)), self.blocks(w, 1, 1, 4))
        for t in range(3):
            self.sibling(w, t, j, 2)

    def finish(self, like):
        self.wait_sent("first", like.at[0, pl.ds(0, 3 * K)])
        self.wait_sent("second", like.at[pl.ds(0, 3)])
        self.wait_sent("third", like.at[pl.ds(0, 12)])
        self.wait_sent("share", like.at[pl.ds(0, 16)])

    def take(self, name, w, *more):
        step = {
            "first": self.first_start,
            "line": self.first_end,
            "plane": self.second_pass,
            "planed": self.second_end,
            "pass": self.third_pass,
            "far": self.third_end,
            "share": self.sibling_end,
        }[name]
        step(w, *more)


class Sum(Links):
    def __init__(self, stages, send, recv):
        super().__init__(send, recv)
        self.stages = stages
        self.half = K // 2

    def spread(self, stage, parts):
        for delta in (2, 1, 3):
            for axis, copies in parts:
                for core, source, target in copies:
                    self.copy(stage, stage, source, target, self.device(axis, delta, core)).start()

    def begin(self, matrix):
        parts = []
        for t in range(3):
            first, rows = GRAM_ROWS[t]
            axis = ORDER[t][0]
            target = self.stages[0].at[self.pos[axis] * 2 + self.core, pl.ds(first, rows)]
            copies = []
            for core in (self.core, 1 - self.core):
                start = pl.multiple_of(core * self.half + first, 8)
                copies.append((core, matrix.at[pl.ds(start, rows)], target))
            target[...] = copies[0][1][...]
            self.copy(0, 0, copies[1][1], target, self.device()).start()
            parts.append((axis, copies))
        self.spread(0, parts)

    def stage_start(self, stage, value):
        parts = []
        for t in range(3):
            first, rows = GRAM_ROWS[t]
            axis = ORDER[t][stage]
            slot = self.pos[axis] if stage == 1 else self.core * RING + self.pos[axis]
            own = self.stages[stage].at[slot, pl.ds(first, rows)]
            own[...] = value[first : first + rows]
            if stage == 2:
                self.copy(2, 2, own, own, self.device()).start()
            cores = (self.core,) if stage == 1 else (self.core, 1 - self.core)
            parts.append((axis, [(core, own, own) for core in cores]))
        self.spread(stage, parts)

    def stage_end(self, stage):
        slots = self.stages[stage]
        count = slots.shape[0]
        self.wait(stage, slots.at[pl.ds(0, count - 1)])
        sums = [slots[2 * i] + slots[2 * i + 1] for i in range(count // 2)]
        return [sums[2 * i] + sums[2 * i + 1] for i in range(count // 4)]

    def take(self, step):
        parts = self.stage_end(step)
        if step == 0:
            self.stage_start(1, parts[0] + parts[1])
        elif step == 1:
            self.stage_start(2, parts[0])
        else:
            self.total = jnp.concatenate(parts, axis=0)

    def finish(self):
        for stage, slots in enumerate(self.stages):
            self.wait_sent(stage, slots.at[pl.ds(0, slots.shape[0] - 1)])


def product(left, right, left_dim, right_dim):
    dims = (((left_dim,), (right_dim,)), ((), ()))
    return lax.dot_general(left, right, dims, precision=HIGHEST, preferred_element_type=jnp.float32)


def factor_inverse(matrix, result, panel=32, pivots=8):
    ids = [lax.broadcasted_iota(jnp.int32, (K, K), dim) for dim in (0, 1)]
    side = jnp.where(ids[0] == ids[1], 1.0, 0.0)
    row = lax.broadcasted_iota(jnp.int32, (panel, K), 0)
    lane = lax.broadcasted_iota(jnp.int32, (panel, K), 1)
    uppers, inverses = [], []
    for first in range(0, K, panel):
        a, w = matrix[:panel], side[:panel]
        done_a, done_w = [], []
        for j in range(0, panel, pivots):
            span, left = range(pivots), panel - j
            at = first + j
            cols = [jnp.broadcast_to(a[:, at + q : at + q + 1], (left, K)) for q in span]
            row_a, row_w = [a[q : q + 1] for q in span], [w[q : q + 1] for q in span]
            small = [[cols[k][q : q + 1] for k in span] for q in span]
            below = left > pivots
            if below:
                cols, a, w = [col[pivots:] for col in cols], a[pivots:], w[pivots:]
            for q in span:
                inverse = 1.0 / small[q][q]
                ratio = {k: small[q][k] * inverse for k in range(q + 1, pivots)}
                for k in range(q + 1, pivots):
                    for m in range(k, pivots):
                        small[k][m] = small[k][m] - ratio[k] * small[q][m]
                    row_a[k] = row_a[k] - ratio[k] * row_a[q]
                    row_w[k] = row_w[k] - ratio[k] * row_w[q]
                if below:
                    weight = cols[q] * inverse
                    for k in range(q + 1, pivots):
                        cols[k] = cols[k] - cols[q] * ratio[k]
                    a = a - weight * row_a[q]
                    w = w - weight * row_w[q]
                root = lax.rsqrt(small[q][q])
                done_a.append(row_a[q] * root)
                done_w.append(row_w[q] * root)
        a = jnp.where(lane >= row + first, jnp.concatenate(done_a, axis=0), 0.0)
        w = jnp.concatenate(done_w, axis=0)
        uppers.append(a)
        inverses.append(w)
        if first + panel < K:
            rest = a[:, first + panel :]
            matrix = matrix[panel:] - product(rest, a, 0, 0)
            side = side[panel:] - product(rest, w, 0, 0)
        yield
    result.extend((jnp.concatenate(uppers, axis=0), jnp.concatenate(inverses, axis=0)))


def kernel(
    cols_hbm,
    live_hbm,
    tiles_hbm,
    degree_hbm,
    basis_hbm,
    image_hbm,
    sum_hbm,
    cols,
    live,
    degree,
    basis,
    tiles,
    a0,
    a1,
    a2,
    a3,
    b0,
    b1,
    b2,
    b3,
    scale,
    total,
    gram,
    summed,
    one_first,
    one_second,
    one_third,
    two_first,
    two_second,
    two_third,
    load_sem,
    send_a,
    recv_a,
    send_b,
    recv_b,
    send_g,
    recv_g,
    send_h,
    recv_h,
):
    items = float(BLK * 2 * RING**3)
    first = Gather((a0, a1, a2, a3), send_a, recv_a)
    second = Gather((b0, b1, b2, b3), send_b, recv_b)
    gram_one = Sum((one_first, one_second, one_third), send_g, recv_g)
    gram_two = Sum((two_first, two_second, two_third), send_h, recv_h)
    pos, core = first.pos, first.core

    barrier = pltpu.get_barrier_semaphore()
    near = [first.device()] + [
        first.device(axis, delta, c)
        for c in (core, 1 - core)
        for axis in range(3)
        for delta in (1, 2, 3)
    ]
    for device in near:
        pl.semaphore_signal(barrier, inc=1, device_id=device, device_id_type=MESH)
    pairs = [(degree_hbm, degree), (basis_hbm, basis), (cols_hbm, cols), (live_hbm, live)]
    pairs += [(tiles_hbm.at[pl.ds(8 * i, 8)], tiles.at[pl.ds(8 * i, 8)]) for i in range(4)]
    loads = [pltpu.make_async_copy(*pair, load_sem.at[i]) for i, pair in enumerate(pairs)]
    for load in loads:
        load.start()

    def place(waves, w, value):
        waves[w][pos[0], pos[1], pos[2], core] = value.astype(jnp.bfloat16)

    loads[0].wait()
    for i in range(BLK // K):
        row_scale = 1.0 / jnp.sqrt(degree[pl.ds(i * K, K)].astype(jnp.float32))
        scale[pl.ds(i * K, K)] = jnp.broadcast_to(row_scale.reshape(1, K), (K, K)).T
    loads[1].wait()
    for w in range(WAVES):
        rows = pl.ds(w * DEPTH, DEPTH)
        place(first.waves, w, scale[rows] * basis[rows].astype(jnp.float32))
    pl.semaphore_wait(barrier, len(near))

    def multiply(waves, w, groups, rows=pl.ds(0, BLK), size=GROUP):
        @pl.loop(*groups)
        def _(group):
            parts = []
            for u in range(size):
                slot = group * size + u
                col = cols[slot]
                picked = waves[w][
                    col // 32, lax.rem(col // 8, 4), lax.rem(col // 2, 4), lax.rem(col, 2)
                ]
                picked = jnp.where(slot < live[0], picked, jnp.zeros_like(picked))
                tile = tiles[slot, rows, pl.ds(w * DEPTH, DEPTH)]
                parts.append(jnp.dot(tile, picked, preferred_element_type=jnp.float32))
            while len(parts) > 1:
                parts = [left + right for left, right in zip(parts[::2], parts[1::2])]
            total[rows] += parts[0]

    total[...] = jnp.zeros_like(total)
    for name, *more in ROUND_ONE:
        if name == "multiply":
            multiply(first.waves, more[0], more[1:])
        elif name == "loaded":
            for load in loads[2:]:
                load.wait()
        else:
            first.take(name, *more)

    def half_image(half):
        rows = pl.ds(half * (BLK // 2), BLK // 2)
        multiply(first.waves, WAVES - 1, (0, 1), rows, SLOTS)
        image = total[rows] * scale[rows]
        total[rows] = image
        image = scale[rows] * image
        for w in range(WAVES // 2):
            place(second.waves, half * (WAVES // 2) + w, image[w * DEPTH : (w + 1) * DEPTH])

    factors = []
    half_image(0)
    for name, *more in ROUND_TWO:
        if name == "half":
            half_image(1)
        elif name == "gram":
            image = total[...]
            total[...] = jnp.zeros_like(total)
            gram[...] = product(image, image, 0, 0) * (1.0 / items)
            gram_one.begin(gram)
        elif name == "sum":
            gram_one.take(more[0])
        elif name == "eliminate":
            if more[0] == 0:
                elimination = factor_inverse(gram_one.total, factors)
            next(elimination)
        elif name == "multiply":
            multiply(second.waves, more[0], more[1:])
        else:
            second.take(name, *more)
    next(elimination, None)
    raw = total[...] * scale[...]
    image = product(raw, factors[1], 1, 1)
    total[...] = image
    out = pltpu.make_async_copy(total, image_hbm, load_sem.at[0])
    out.start()
    gram_one.finish()
    gram[...] = product(image, image, 0, 0) * (1.0 / items)
    gram_two.begin(gram)
    for step in range(3):
        gram_two.take(step)
    summed[...] = gram_two.total
    out_sum = pltpu.make_async_copy(summed, sum_hbm, load_sem.at[1])
    out_sum.start()
    first.finish(tiles)
    second.finish(tiles)
    gram_two.finish()
    out.wait()
    out_sum.wait()


def finish(image, gram, leading, factor):
    factors = []
    for _ in factor_inverse(gram[...], factors, panel=64):
        pass
    upper, inverse = factors
    factor[...] = upper.T
    leading[...] = product(image[...], inverse, 1, 1)


def local(tile_data, tile_col, live_count, degree, start_basis):
    vmem, anywhere = pl.BlockSpec(memory_space=pltpu.VMEM), pl.BlockSpec(memory_space=pl.ANY)
    wave = pltpu.VMEM((RING, RING, RING, 2, DEPTH, K), jnp.bfloat16)
    sums = [
        pltpu.VMEM((2 * RING, K // 2, K), jnp.float32),
        pltpu.VMEM((RING, K // 2, K), jnp.float32),
        pltpu.VMEM((2 * RING, K // 2, K), jnp.float32),
    ]
    dma = pltpu.SemaphoreType.DMA
    rows = jax.ShapeDtypeStruct((BLK, K), jnp.float32)
    square = jax.ShapeDtypeStruct((K, K), jnp.float32)
    image, gram = pl.pallas_call(
        kernel,
        out_shape=(rows, square),
        in_specs=[anywhere] * 5,
        out_specs=(anywhere, anywhere),
        scratch_shapes=[
            pltpu.SMEM((SLOTS,), jnp.int32),
            pltpu.SMEM((1,), jnp.int32),
            pltpu.VMEM((BLK,), jnp.int32),
            pltpu.VMEM((BLK, K), jnp.bfloat16),
            pltpu.VMEM((SLOTS, BLK, BLK), jnp.bfloat16),
            *[wave] * (2 * WAVES),
            pltpu.VMEM((BLK, K), jnp.float32),
            pltpu.VMEM((BLK, K), jnp.float32),
            pltpu.VMEM((K, K), jnp.float32),
            pltpu.VMEM((K, K), jnp.float32),
            *sums * 2,
            dma((8,)),
            *[dma((SENDS,)), dma((RECEIPTS,))] * 2,
            *[dma((SUMS,))] * 4,
        ],
        compiler_params=pltpu.CompilerParams(
            collective_id=0, has_side_effects=True, vmem_limit_bytes=58 * 2**20
        ),
        name="two_rounds",
    )(tile_col, live_count, tile_data, degree, start_basis)
    return pl.pallas_call(
        finish,
        out_shape=(rows, square),
        in_specs=[vmem] * 2,
        out_specs=(vmem, vmem),
        name="finish",
    )(image, gram)


def solution(mesh):
    placed = (
        P(("hst", "chip"), None, None),
        P(("hst", "chip")),
        P(("hst", "chip")),
        P(("hst", "chip")),
        P(("hst", "chip"), None),
    )
    return jax.shard_map(
        local,
        mesh=mesh,
        in_specs=placed,
        out_specs=(P(("hst", "chip"), None), P()),
        check_vma=False,
    )
```
